512 devices in a mesh: ctx: 16 (over y, x_hi, core), exp: 32 (over z, x_lo).
Axes of the slice: x: 4 (x_hi: 2, x_lo: 2; x = x_hi * 2 + x_lo), y: 4, z: 16, core: 2. Of those that a mesh axis runs over, the one named last changes fastest.
Arguments:
- resid: bfloat16 [32, 256, 4096], P('exp', 'ctx'), may hold values from -4 to 4
- query: bfloat16 [32, 256, 4096], P('exp', 'ctx'), may hold values from -10 to 10
- key_new: bfloat16 [32, 256, 256], P('exp', 'ctx'), may hold values from -6 to 6
- value_new: bfloat16 [32, 256, 256], P('exp', 'ctx'), may hold values from -6 to 6
- cache_key: bfloat16 [32, 2048, 256], P('exp', 'ctx'), may hold values from -240 to 240
- cache_value: bfloat16 [32, 2048, 256], P('exp', 'ctx'), may hold values from -6 to 6
- cache_len: int32 [32], P('exp'), may hold values from 512 to 2048
- block_of: int32 [16], replicated, may hold values from 0 to 15, each once
- out_proj: bfloat16 [4096, 4096], P(None, 'ctx'), may hold values from -0.09375 to 0.09375
- norm_gain: float32 [4096], replicated, may hold values from 0.1 to 1.9
- routes: int32 [32, 256, 8], P('exp', 'ctx'), may hold values from 0 to 127, as said below
- route_logits: float32 [32, 256, 8], P('exp', 'ctx'), may hold values from -12 to 304
- w_gate: bfloat16 [32, 1536, 4096], P('exp', 'ctx'), may hold values from -0.25 to 0.25
- w_up: bfloat16 [32, 1536, 4096], P('exp', 'ctx'), may hold values from -0.25 to 0.25
- w_down: bfloat16 [32, 1536, 4096], P('exp', None, 'ctx'), may hold values from -0.375 to 0.375
Outputs:
- layer_out: bfloat16 [32, 256, 4096], P('exp', 'ctx')
The draws below stay inside these ranges and needn't reach their ends.
Inputs may be any that keep to these rules, and one draw needn't show every extreme that they name: `routes`: each row names 8 different expert numbers of 0 to 127; only numbers below 32 are experts of this layer slice; among the rows of one device no number appears more than 2 times, and 2 is reached on every device. `block_of`: a permutation.
All inputs are finite; a program needn't handle non-finite values.
Results may differ from the reference program's by a relative error of at most 0.015.
The reference program's roundings to bfloat16 on the way (of `turned`, `rotated_keys`, `weights`, `mixed`, `stream`, `normed`, `hidden` and `result`) count: a program that leaves them out, or rounds other values in their place, can miss the bound.
Values may be sent and summed in bfloat16 or wider, within the bound.
A program may use at most 128 MiB of HBM per device.

```python
import math
import jax
import jax.numpy as jnp
from jax import lax

D = 4096
FF = 1536
HD = 128
ROUTED = 128
HEADS = 32
KVH = 2
TOPK = 8
CAP = 2
TOK_DEV = 16
CACHE_DEV = 128
REQS = 32
EXPERTS = 32
NEW = 256
CACHE = 2048
N_CTX = 16
N_EXP = 32


def leading_column(key):
    key = jax.random.fold_in(key, 21)
    return jax.random.randint(key, (REQS, NEW), 0, TOPK).astype(jnp.int32)


def draw_cache_key(key, part):
    key = jax.random.fold_in(key, 11)
    first = jax.random.fold_in(key, 0)
    base = jnp.clip(jax.random.normal(first, (REQS, CACHE, KVH * HD), jnp.float32), -5.0, 5.0)
    return base.astype(jnp.bfloat16)


def draw_cache_len(key, part):
    key = jax.random.fold_in(key, 5)
    first, second = jax.random.split(key)
    lowest = CACHE // 4
    highest = CACHE
    values = jax.random.randint(first, (REQS,), lowest, highest + 1)
    order = jax.random.permutation(second, REQS)
    values = values.at[order[0]].set(highest)
    values = values.at[order[1]].set(lowest)
    return values.astype(jnp.int32)


def route_block(key, filled):
    outer_key, pool_key, offset_key, shuffle_key = jax.random.split(key, 4)
    width = TOPK - 2
    pairs = TOK_DEV // 2
    outside = (EXPERTS + jax.random.permutation(outer_key, ROUTED - EXPERTS)).astype(jnp.int32)
    reserved = outside[:TOK_DEV]
    numbers = jnp.arange(ROUTED, dtype=jnp.int32)
    excluded = (numbers == filled) | jnp.any(numbers[:, None] == reserved[None, :], axis=1)
    shuffled = jax.random.permutation(pool_key, ROUTED).astype(jnp.int32)
    order = shuffled[jnp.argsort(excluded[shuffled].astype(jnp.int32), stable=True)]
    sequence = jnp.concatenate([order[:width - 1], filled[None], order[width - 1:]])
    offsets = jax.random.randint(offset_key, (pairs,), 2, TOPK - 2).astype(jnp.int32)
    spans = width + offsets
    starts = jnp.cumsum(spans) - spans
    columns = jnp.arange(width, dtype=jnp.int32)
    first_rows = sequence[starts[:, None] + columns[None, :]]
    second_rows = sequence[(starts + offsets)[:, None] + columns[None, :]]
    rest = jnp.stack([first_rows, second_rows], axis=1).reshape(TOK_DEV, width)
    leader = jnp.repeat(reserved[0::2], 2)
    runner = jnp.repeat(reserved[1::2], 2)
    rows = jnp.concatenate([leader[:, None], runner[:, None], rest], axis=1)
    return rows[jax.random.permutation(shuffle_key, TOK_DEV)]


def draw_routes(key, part):
    leading = leading_column(key)
    key = jax.random.fold_in(key, 3)
    full_key, block_key = jax.random.split(key)
    filled_by_shard = jax.random.randint(full_key, (N_CTX,), 0, EXPERTS).astype(jnp.int32)
    block_keys = jax.random.split(block_key, REQS * N_CTX)
    blocks = jax.vmap(route_block)(block_keys, jnp.tile(filled_by_shard, REQS))
    rows = blocks.reshape(REQS, NEW, TOPK)
    places = (jnp.arange(TOPK, dtype=jnp.int32)[None, None, :] - leading[:, :, None]) % TOPK
    return jnp.take_along_axis(rows, places, axis=2).astype(jnp.int32)


def draw_route_logits(key, part):
    leading = leading_column(key)
    key = jax.random.fold_in(key, 9)
    first, second, third = jax.random.split(key, 3)
    columns = jnp.arange(TOPK, dtype=jnp.int32)[None, None, :]
    is_top = columns == leading[:, :, None]
    is_next = columns == ((leading + 1) % TOPK)[:, :, None]
    close = jax.random.uniform(first, (REQS, NEW, 1), jnp.float32, 1.0, 3.0)
    distant = jax.random.uniform(second, (REQS, NEW, TOPK), jnp.float32, 4.7, 5.7)
    summit = jax.random.uniform(third, (REQS, NEW, 1), jnp.float32, -1.0, 3.0)
    gaps = jnp.where(is_top, 0.0, jnp.where(is_next, close, distant))
    return (summit - gaps).astype(jnp.float32)


def steps_of(stream_key, shape, shards, least, high):
    loudness = 1.0
    for dim, parts in shards:
        steps = jax.random.uniform(jax.random.fold_in(jax.random.fold_in(stream_key, 6), dim), (parts,), jnp.float32, least / len(shards), high / len(shards))
        loudness = loudness * jnp.repeat(jnp.exp(steps), shape[dim] // parts).reshape((-1,) + (1,) * (len(shape) - 1 - dim))
    return loudness


def scatter_about(own_key, shape, scale, reach, cuts=(), kind=jnp.bfloat16):
    array = scale * jax.random.normal(own_key, shape, jnp.float32)
    if cuts:
        array = array * steps_of(own_key, shape, cuts, -0.22, 0.18)
    return jnp.clip(array, -reach, reach).astype(kind)


def setup_inputs(seed: int = 0) -> dict:
    splits = jax.random.split(jax.random.key(seed), 16)
    resid = scatter_about(splits[0], (REQS, NEW, D), 0.5, 4.0, ((0, 32), (1, 16)))
    query = scatter_about(splits[1], (REQS, NEW, HEADS * HD), 2.0, 10.0, ((0, 32), (1, 16)))
    key_new = scatter_about(splits[2], (REQS, NEW, KVH * HD), 1.0, 6.0, ((0, 32), (1, 16)))
    value_new = scatter_about(splits[3], (REQS, NEW, KVH * HD), 1.0, 6.0, ((0, 32), (1, 16)))
    cache_key = draw_cache_key(jax.random.fold_in(splits[15], 71), 0)
    cache_value = scatter_about(splits[5], (REQS, CACHE, KVH * HD), 1.0, 6.0, ((0, 32), (1, 16)))
    cache_len = draw_cache_len(jax.random.fold_in(splits[15], 71), 0)
    block_of = jax.random.permutation(splits[7], N_CTX).astype(jnp.int32)
    out_proj = scatter_about(splits[8], (HEADS * HD, D), (HEADS * HD) ** -0.5, 0.09375, ((1, 16),))
    norm_gain = jnp.clip(1.0 + 0.18 * jax.random.normal(splits[9], (D,), jnp.float32), 0.1, 1.9)
    routes = draw_routes(jax.random.fold_in(splits[15], 71), 0)
    route_logits = draw_route_logits(jax.random.fold_in(splits[15], 71), 0)
    w_gate = scatter_about(splits[12], (EXPERTS, FF, D), (D // 9) ** -0.5, 0.25, ((0, 32), (1, 16)))
    w_up = scatter_about(splits[13], (EXPERTS, FF, D), (D // 9) ** -0.5, 0.25, ((0, 32), (1, 16)))
    w_down = scatter_about(splits[14], (EXPERTS, FF, D), (FF // 6) ** -0.5, 0.375, ((0, 32), (2, 16)))
    return dict(resid=resid, query=query, key_new=key_new, value_new=value_new, cache_key=cache_key, cache_value=cache_value, cache_len=cache_len, block_of=block_of, out_proj=out_proj, norm_gain=norm_gain, routes=routes, route_logits=route_logits, w_gate=w_gate, w_up=w_up, w_down=w_down)


def rotate(vectors, positions):
    half = vectors.shape[-1] // 2
    rates = jnp.exp(jnp.arange(half, dtype=jnp.float32) * (-2.0 * math.log(1000000.0) / vectors.shape[-1]))
    angles = positions.astype(jnp.float32)[:, None] * rates[None, :]
    cosine = jnp.cos(angles)[:, None, :]
    sine = jnp.sin(angles)[:, None, :]
    first = vectors[..., :half]
    second = vectors[..., half:]
    return jnp.concatenate([first * cosine - second * sine, second * cosine + first * sine], axis=-1)

def reference(resid, query, key_new, value_new, cache_key, cache_value, cache_len, block_of, out_proj, norm_gain, routes, route_logits, w_gate, w_up, w_down):
    fresh = TOK_DEV * N_CTX
    stored = CACHE_DEV * N_CTX
    sharing = HEADS // KVH
    scale = HD ** (-0.5)
    counter = jnp.arange(fresh, dtype=jnp.int32)
    offsets = block_of.astype(jnp.int32)[counter // TOK_DEV] * TOK_DEV + counter % TOK_DEV

    def attend(inputs):
        queries, new_keys, new_values, old_keys, old_values, length = inputs
        positions = length + offsets
        turned = rotate(queries.astype(jnp.float32).reshape(fresh, HEADS, HD), positions).astype(jnp.bfloat16)
        turned = turned.reshape(fresh, KVH, sharing, HD).transpose(1, 0, 2, 3).reshape(KVH, fresh * sharing, HD)
        rotated_keys = rotate(new_keys.astype(jnp.float32).reshape(fresh, KVH, HD), positions)
        rotated_keys = rotated_keys.astype(jnp.bfloat16).reshape(fresh, KVH * HD)
        all_keys = jnp.concatenate([old_keys, rotated_keys], axis=0).reshape(stored + fresh, KVH, HD)
        all_values = jnp.concatenate([old_values, new_values], axis=0).reshape(stored + fresh, KVH, HD)
        scores = jnp.einsum('hqd,khd->hqk', turned.astype(jnp.float32), all_keys.astype(jnp.float32)) * scale
        row_positions = jnp.repeat(positions, sharing)
        cached = jnp.broadcast_to((jnp.arange(stored, dtype=jnp.int32) < length)[None, :], (fresh * sharing, stored))
        causal = positions[None, :] <= row_positions[:, None]
        valid = jnp.concatenate([cached, causal], axis=1)[None]
        scores = jnp.where(valid, scores, -1e+30)
        peak = lax.optimization_barrier(jnp.max(scores, axis=2, keepdims=True))
        weights = jnp.where(valid, jnp.exp(scores - peak), 0.0)
        total = lax.optimization_barrier(jnp.sum(weights, axis=2, keepdims=True))
        rounded_weights = lax.optimization_barrier(weights.astype(jnp.bfloat16)).astype(jnp.float32)
        mixed = jnp.einsum('hqk,khd->hqd', rounded_weights, all_values.astype(jnp.float32)) / total
        mixed = mixed.astype(jnp.bfloat16).reshape(KVH, fresh, sharing, HD).transpose(1, 0, 2, 3)
        return mixed.reshape(fresh, HEADS * HD)
    mixed = lax.map(attend, (query, key_new, value_new, cache_key, cache_value, cache_len))
    attention = jnp.dot(mixed.reshape(-1, HEADS * HD), out_proj, preferred_element_type=jnp.float32)
    rounded = lax.optimization_barrier((resid.reshape(-1, D).astype(jnp.float32) + attention).astype(jnp.bfloat16))
    stream = rounded.astype(jnp.float32)
    normed = (stream * lax.rsqrt(lax.optimization_barrier(jnp.mean(stream * stream, axis=1, keepdims=True)) + 1e-06) * norm_gain).astype(jnp.bfloat16)
    shares = jax.nn.softmax(route_logits.reshape(-1, TOPK).astype(jnp.float32), axis=1)
    chosen = routes.reshape(-1, TOPK).astype(jnp.int32)
    most_rows = N_CTX * N_EXP * CAP

    def serve(total, inputs):
        expert, gate_matrix, up_matrix, down_matrix = inputs
        hits = chosen == expert
        share = lax.optimization_barrier(jnp.sum(jnp.where(hits, shares, 0.0), axis=1))
        taken = jnp.any(hits, axis=1)
        picked = jnp.nonzero(taken, size=most_rows, fill_value=0)[0].astype(jnp.int32)
        live = jnp.arange(most_rows, dtype=jnp.int32) < jnp.sum(taken.astype(jnp.int32))
        rows = normed[picked]
        gate = jnp.dot(rows, gate_matrix.T, preferred_element_type=jnp.float32)
        upward = jnp.dot(rows, up_matrix.T, preferred_element_type=jnp.float32)
        hidden = (jax.nn.silu(gate) * upward).astype(jnp.bfloat16)
        result = jnp.dot(hidden, down_matrix, preferred_element_type=jnp.float32).astype(jnp.bfloat16)
        factor = jnp.where(live, share[picked], 0.0)
        return (total.at[picked].add(result.astype(jnp.float32) * factor[:, None]), None)
    summed, unused = lax.scan(serve, jnp.zeros((stream.shape[0], D), jnp.float32), (jnp.arange(EXPERTS, dtype=jnp.int32), w_gate, w_up, w_down))
    return (stream + summed).astype(jnp.bfloat16).reshape(REQS, fresh, D)
```

```python
import math

import jax
import jax.numpy as jnp
import numpy as np
from jax import lax
from jax.experimental import pallas as pl
from jax.experimental.pallas import tpu as pltpu
from jax.sharding import PartitionSpec as P

MESH = pl.DeviceIdType.MESH
BF = jnp.bfloat16
F32 = jnp.float32
HD = 128
TOK = 16
CACHED = 128
KEYS = TOK + CACHED
GROUP = 16
PLANES = 8
WIDE = 512
NEXP = 32
UNITS = 96
OFFSETS = ((0, 1, -1, 2), (8, 7, -7, -6), (6, 5, -5, -4), (4, 3, -3, -2))
CHUNKS = len(OFFSETS)
PER = 8
ROWS = PER * 2 * PLANES
YS = (2, 6, 4)
NEG = -1e30
SENDS = 288
RECVS = 320


def iota(shape, axis):
    return lax.broadcasted_iota(jnp.int32, shape, axis)


def onehot(condition):
    return jnp.where(condition, 1.0, 0.0).astype(BF)


def dot(a, b):
    return jnp.dot(a, b, preferred_element_type=F32)


def dot_t(a, b):
    return lax.dot_general(a, b, (((1,), (1,)), ((), ())), preferred_element_type=F32)


def thirds(x):
    high = x.astype(BF)
    rest = x - high.astype(F32)
    middle = rest.astype(BF)
    return high, middle, (rest - middle.astype(F32)).astype(BF)


def kernel(
    length_ref,
    block_ref,
    rates_ref,
    resid_ref,
    query_ref,
    key_new_ref,
    value_new_ref,
    cache_key_ref,
    cache_value_ref,
    gain_ref,
    routes_ref,
    logits_ref,
    out_proj_hbm,
    gate_hbm,
    up_hbm,
    down_hbm,
    out_ref,
    q_buf,
    q_stage,
    kv,
    kv_stage,
    score_buf,
    peak_buf,
    mix,
    w_out,
    part_send,
    part_recv,
    proj_send,
    attn,
    stream_buf,
    info,
    z_send,
    z_recv,
    rows_buf,
    w_gate,
    w_up,
    w_down,
    hid,
    ret_send,
    ret,
    fin_send,
    fin,
    send_sems,
    recv_sems,
    local_sems,
):
    ctx = lax.axis_index("ctx")
    ex = lax.axis_index("exp")
    core, p = lax.rem(ctx, 2), lax.div(ctx, 2)
    y, h = lax.div(p, 2), lax.rem(p, 2)
    z, low = lax.div(ex, 2), lax.rem(ex, 2)
    other = 1 - core
    ys = {0: y, 2: y + 1 - 2 * lax.rem(y, 2), 4: lax.rem(y + 2, 4), 6: 3 - y}
    peer = [2 * ys[i & 6] + ((1 - h) if i & 1 else h) for i in range(PLANES)]
    partner = {"ctx": 2 * p + other}

    def plane(i):
        return {"ctx": 2 * peer[i] + core}

    slots = []
    for chunk in OFFSETS:
        for d in chunk:
            for flip in (0, 1):
                slots.append((d, flip))

    def exp_at(d, flip):
        return 2 * lax.rem(z + d + 16, 16) + (1 - low if flip else low)

    started = []
    counts = {"send": 0, "recv": 0, "local": 0}

    def take(kind, n):
        first = counts[kind]
        counts[kind] += n
        assert counts[kind] <= {"send": SENDS, "recv": RECVS, "local": 8}[kind]
        return first

    def send(src, dst, recv, device):
        copy = pltpu.make_async_remote_copy(
            src_ref=src,
            dst_ref=dst,
            send_sem=send_sems.at[take("send", 1)],
            recv_sem=recv_sems.at[recv],
            device_id=device,
            device_id_type=MESH,
        )
        copy.start()
        started.append(copy)

    def arrive(dst, recv):
        pltpu.make_async_remote_copy(
            src_ref=dst,
            dst_ref=dst,
            send_sem=send_sems.at[0],
            recv_sem=recv_sems.at[recv],
            device_id=partner,
            device_id_type=MESH,
        ).wait_recv()

    class Gather:
        def __init__(self, at):
            self.at = at
            self.base = take("recv", 2 * PLANES)

        def put(self, source, half, i):
            ref = self.at(source, half)
            send(ref, ref, self.base + 2 * source + half, plane(i))

        def wait(self, i, half):
            arrive(self.at(peer[i], half), self.base + 2 * peer[i] + half)

        def start(self, half):
            for i in (1,) + YS if half == 0 else YS + (1,):
                self.put(p, half, i)

        def forward(self):
            self.wait(1, 0)
            for i in YS:
                self.put(peer[1], 0, i)
            for i in YS:
                self.wait(i, 1)
                self.put(peer[i], 1, 1)

        def finish(self):
            for i in YS:
                self.wait(i, 0)
            self.wait(1, 1)
            for i in YS:
                self.wait(i + 1, 0)
                self.wait(i + 1, 1)

    barrier = pltpu.get_barrier_semaphore()
    pl.semaphore_signal(barrier, inc=1, device_id=partner, device_id_type=MESH)
    for i in range(1, PLANES):
        pl.semaphore_signal(barrier, inc=1, device_id=plane(i), device_id_type=MESH)
    for d, flip in slots[1:]:
        pl.semaphore_signal(
            barrier, inc=1, device_id={"exp": exp_at(d, flip)}, device_id_type=MESH
        )

    mine96 = pl.ds(pl.multiple_of(core * UNITS, 16), UNITS)
    head192 = pl.ds(0, 2 * UNITS)
    own_half = pl.ds(pl.multiple_of(core * 2048, 16), 2048)
    other_half = pl.ds(pl.multiple_of(other * 2048, 16), 2048)
    locals_ = []
    for src, dst in (
        (out_proj_hbm.at[own_half], w_out.at[core]),
        (gate_hbm, w_gate.at[mine96]),
        (up_hbm, w_up.at[mine96]),
        (down_hbm, w_down.at[core, :, head192]),
    ):
        copy = pltpu.make_async_copy(src, dst, local_sems.at[take("local", 1)])
        copy.start()
        locals_.append(copy)

    first = core == 0
    length = length_ref[0]
    block_mine = block_ref[ctx]
    block_other = block_ref[2 * p + other]
    position = (iota((TOK, HD), 0) + (length + block_mine * TOK)).astype(F32)
    angles = position * rates_ref[...]
    cosine = jnp.cos(angles)
    sine = jnp.where(iota((TOK, HD), 1) < HD // 2, -1.0, 1.0) * jnp.sin(angles)

    def rope(v):
        v = v.astype(F32)
        return (v * cosine + pltpu.roll(v, HD // 2, 1) * sine).astype(BF)

    for g in range(GROUP):
        low_head = rope(query_ref[:, g * HD : (g + 1) * HD])
        high_head = rope(query_ref[:, (GROUP + g) * HD : (GROUP + g + 1) * HD])
        q_buf[g * TOK : (g + 1) * TOK] = jnp.where(first, low_head, high_head)
        q_stage[g * TOK : (g + 1) * TOK] = jnp.where(first, high_head, low_head)
    for which, cached_ref, new_ref in ((0, cache_key_ref, key_new_ref), (1, cache_value_ref, value_new_ref)):
        old = [cached_ref[:, n * HD : (n + 1) * HD] for n in (0, 1)]
        new = [new_ref[:, n * HD : (n + 1) * HD] for n in (0, 1)]
        if which == 0:
            new = [rope(v) for v in new]
        kv[p, 0, which, :CACHED] = jnp.where(first, old[0], old[1])
        kv[p, 0, which, CACHED:] = jnp.where(first, new[0], new[1])
        kv_stage[which, :CACHED] = jnp.where(first, old[1], old[0])
        kv_stage[which, CACHED:] = jnp.where(first, new[1], new[0])

    logits = logits_ref[...]
    powers = jnp.exp(logits - jnp.max(logits, axis=1, keepdims=True))
    shares = powers / jnp.sum(powers, axis=1, keepdims=True)
    routes = routes_ref[...]
    lane = iota((TOK, 128), 1)
    token = iota((TOK, 128), 0)
    taken = jnp.zeros((TOK, 128), F32)
    share = jnp.zeros((TOK, 128), F32)
    for x in range(8):
        hit = routes[:, x : x + 1] == lane
        taken = jnp.where(hit, 1.0, taken)
        share = share + jnp.where(hit, shares[:, x : x + 1], 0.0)
    rank = taken
    for step in (1, 2, 4, 8):
        rank = rank + jnp.where(token >= step, pltpu.roll(rank, step, 0), 0.0)
    row_of = jnp.where(taken > 0.0, rank - 1.0, -1.0)
    info[p, 0] = row_of
    info[p, 1] = share

    pl.semaphore_wait(barrier, PLANES + len(slots) - 1)

    kv_gather = Gather(lambda source, half: kv.at[source, half])
    pair_kv, pair_q = take("recv", 1), take("recv", 1)
    send(kv_stage, kv.at[p, 1], pair_kv, partner)
    kv_gather.start(0)
    q_theirs = q_buf.at[pl.ds(GROUP * TOK, GROUP * TOK)]
    send(q_stage, q_theirs, pair_q, partner)
    arrive(kv.at[p, 1], pair_kv)
    kv_gather.start(1)
    pair_weights = [take("recv", 1) for _ in range(4)]
    send(out_proj_hbm.at[other_half], w_out.at[core], pair_weights[0], partner)
    send(gate_hbm, w_gate.at[mine96], pair_weights[1], partner)
    send(up_hbm, w_up.at[mine96], pair_weights[2], partner)
    send(down_hbm, w_down.at[core, :, head192], pair_weights[3], partner)
    info_base = take("recv", PLANES)
    for i in range(1, PLANES):
        send(info.at[p], info.at[p], info_base + p, plane(i))

    row8 = jnp.concatenate([row_of.astype(BF)] * PLANES, axis=0)
    s_row, s_lane = iota((512, 128), 0), iota((512, 128), 1)
    spread = dot_t(onehot((s_row >> 4) == s_lane), row8)
    select = onehot(
        (spread == ((s_row >> 3) & 1).astype(F32)) & ((s_row & 7) == (s_lane >> 4))
    )

    scale = HD ** (-0.5)
    arrive(q_theirs, pair_q)
    q_rows = 2 * GROUP * TOK
    QB = 128

    key_lane = iota((1, 256), 1)

    def score(slot, keys, visible_of):
        def step(rb, carry):
            rows = pl.ds(pl.multiple_of(rb * QB, QB), QB)
            s = dot_t(q_buf[rows], keys) * scale
            s = jnp.where(visible_of(rb), s, NEG)
            score_buf[slot, rows] = s
            top = jnp.maximum(s[:, :128], s[:, 128:])
            peak_buf[rows] = jnp.maximum(peak_buf[rows], top)
            return carry

        lax.fori_loop(0, q_rows // QB, step, 0)

    def score_cached(i):
        source = peer[i]
        keys = jnp.concatenate([kv[source, 0, 0, :CACHED], kv[source, 1, 0, :CACHED]], axis=0)
        near = (2 * source + core) * CACHED
        far = (2 * source + other) * CACHED
        slot = jnp.where(key_lane < CACHED, near + key_lane, far + key_lane - CACHED)
        visible = slot < length
        score(source, keys, lambda rb: visible)

    peak_buf[...] = jnp.full((q_rows, 128), NEG, F32)
    score_cached(0)
    kv_gather.forward()
    kv_gather.finish()
    for i in (1,) + YS + (3, 7, 5):
        score_cached(i)
    new_keys = jnp.concatenate(
        [kv[s, o, 0, CACHED:] for s in range(PLANES) for o in (0, 1)], axis=0
    )
    new_values = jnp.concatenate(
        [kv[s, o, 1, CACHED:] for s in range(PLANES) for o in (0, 1)], axis=0
    )
    key_offset = jnp.zeros((1, 256), jnp.int32)
    for s in range(PLANES):
        for o in (0, 1):
            block = block_ref[2 * s + (core if o == 0 else other)]
            key_offset = jnp.where((key_lane >> 4) == 2 * s + o, block * TOK, key_offset)
    key_offset = key_offset + (key_lane & 15)

    def causal(rb):
        block = jnp.where(rb < 2, block_mine, block_other)
        return key_offset <= (iota((QB, 256), 0) & 15) + block * TOK

    score(PLANES, new_keys, causal)

    def weigh(rb, carry):
        rows = pl.ds(pl.multiple_of(rb * QB, QB), QB)
        peak = jnp.max(peak_buf[rows], axis=1, keepdims=True)
        total = jnp.zeros((QB, 128), F32)
        mixed = jnp.zeros((QB, HD), F32)
        for s in range(PLANES + 1):
            weights = jnp.exp(score_buf[s, rows] - peak)
            total = total + weights[:, :128] + weights[:, 128:]
            if s < PLANES:
                values = jnp.concatenate([kv[s, 0, 1, :CACHED], kv[s, 1, 1, :CACHED]], axis=0)
            else:
                values = new_values
            mixed = mixed + dot(weights.astype(BF), values)
        mixed = (mixed / jnp.sum(total, axis=1, keepdims=True)).astype(BF)
        q_buf[rows] = mixed
        return carry

    lax.fori_loop(0, q_rows // QB, weigh, 0)
    for o in (0, 1):
        for g in range(GROUP):
            r = (o * GROUP + g) * TOK
            mix[o, p, :, g * HD : (g + 1) * HD] = q_buf[r : r + TOK]

    mix_gather = Gather(lambda source, half: mix.at[half, source])
    mix_gather.start(0)
    mix_gather.start(1)
    mix_gather.forward()
    locals_[0].wait()
    arrive(w_out.at[other], pair_weights[0])
    mix_gather.finish()

    def project(o):
        left = mix[o].reshape(PLANES * TOK, 2048)
        return [dot(left, w_out[half]) for half in (0, 1)]

    pair_part = take("recv", 1)
    theirs = project(1)
    part_send[0] = theirs[0]
    part_send[1] = theirs[1]
    send(part_send, part_recv, pair_part, partner)
    ours = project(0)
    arrive(part_recv, pair_part)
    for half in (0, 1):
        block = (ours[half] + part_recv[half]).astype(BF).reshape(PLANES, TOK, 256)
        proj_send[:, :, half * 256 : (half + 1) * 256] = block
    attn_base = take("recv", PLANES)
    for i in YS + (1, 3, 7, 5):
        send(proj_send.at[peer[i]], attn.at[p], attn_base + p, plane(i))
    attn[p] = proj_send[p]
    for i in range(1, PLANES):
        arrive(attn.at[peer[i]], attn_base + peer[i])

    square = jnp.zeros((TOK, 1), F32)
    streams = []
    for j in range(PLANES):
        cols = slice(j * WIDE, (j + 1) * WIDE)
        v = (resid_ref[:, cols].astype(F32) + attn[j].astype(F32)).astype(BF)
        stream_buf[j] = v
        v = v.astype(F32)
        streams.append(v)
        square = square + jnp.sum(v * v, axis=1, keepdims=True)
    inverse = lax.rsqrt(square * (1.0 / (PLANES * WIDE)) + 1e-06)
    normed = jnp.concatenate(
        [
            (streams[j] * inverse * gain_ref[:, j * WIDE : (j + 1) * WIDE]).astype(BF)
            for j in range(PLANES)
        ],
        axis=0,
    )
    z_send[...] = dot(select, normed).astype(BF).reshape(NEXP, 16, WIDE)

    z_base = take("recv", len(slots))
    z_recv[0] = z_send[ex]
    for n, (d, flip) in enumerate(slots):
        if n > 0:
            to = exp_at(d, flip)
            send(z_send.at[to], z_recv.at[n], z_base + n, {"exp": to})

    for copy in locals_[1:]:
        copy.wait()
    theirs96 = pl.ds(pl.multiple_of(other * UNITS, 16), UNITS)
    arrive(w_gate.at[theirs96], pair_weights[1])
    arrive(w_up.at[theirs96], pair_weights[2])
    arrive(w_down.at[other, :, head192], pair_weights[3])
    w_gate[192:] = w_gate[128:192]
    w_up[192:] = w_up[128:192]
    for o in (0, 1):
        w_down[o, :, 192:] = w_down[o, :, 128:192]

    r_, c_ = iota((128, 128), 0), iota((128, 128), 1)
    to_blocks = onehot(((r_ >> 4) == (c_ & 7)) & ((r_ & 15) == (c_ >> 3)))
    to_requests = onehot(
        ((r_ >> 4) == ((c_ >> 1) & 7)) & (((r_ >> 1) & 7) == (c_ >> 4)) & ((r_ & 1) == (c_ & 1))
    )
    ret_base = take("recv", len(slots))
    row_gathers = [
        Gather(lambda source, half, q=q: rows_buf.at[q, source, pl.ds(4 * half, 4)])
        for q in range(CHUNKS)
    ]
    hid_gathers = [
        Gather(lambda source, half, q=q: hid.at[q, source, pl.ds(UNITS * half, UNITS)])
        for q in range(CHUNKS)
    ]

    def gather_rows(q):
        for n in range(q * PER, (q + 1) * PER):
            if n > 0:
                arrive(z_recv.at[n], z_base + n)
        block = z_recv[q * PER : (q + 1) * PER].reshape(128, WIDE)
        rows_buf[q, p] = dot(to_blocks, block).astype(BF).reshape(PLANES, 16, WIDE)
        row_gathers[q].start(0)
        row_gathers[q].start(1)

    def activate(q):
        row_gathers[q].finish()
        gate = jnp.zeros((ROWS, 256), F32)
        upward = jnp.zeros((ROWS, 256), F32)
        for j in range(PLANES):
            rows = rows_buf[q, :, j].reshape(ROWS, WIDE)
            cols = slice(j * WIDE, (j + 1) * WIDE)
            gate = gate + dot_t(rows, w_gate[:, cols])
            upward = upward + dot_t(rows, w_up[:, cols])
        hidden = (gate / (1.0 + jnp.exp(-gate)) * upward).astype(BF)
        tail = hidden[:, 128:]
        left = iota((64, 128), 1) < 64
        hid[q, p, :128] = hidden[:, :128]
        hid[q, p, 128:] = jnp.where(left, tail[:64], tail[64:])
        hid_gathers[q].start(0)
        hid_gathers[q].start(1)

    def finish_rows(q):
        hid_gathers[q].finish()
        left = iota((64, 128), 1) < 64
        result = [jnp.zeros((ROWS, 256), F32) for _ in (0, 1)]
        zero = jnp.zeros((64, 128), BF)
        for s in range(PLANES):
            tail = hid[q, s, 128:]
            tail = jnp.concatenate(
                [jnp.where(left, tail, zero), jnp.where(left, zero, tail)], axis=0
            )
            hidden = jnp.concatenate([hid[q, s, :128], tail], axis=1)
            for o in (0, 1):
                result[o] = result[o] + dot(hidden, w_down[o, s])
        for o in (0, 1):
            block = dot(to_requests, result[o].astype(BF)).astype(BF).reshape(PER, 16, 256)
            ret_send[q * PER : (q + 1) * PER, :, o * 256 : (o + 1) * 256] = block
        for n in range(q * PER, (q + 1) * PER):
            d, flip = slots[n]
            if n > 0:
                send(ret_send.at[n], ret.at[ex], ret_base + n, {"exp": exp_at(-d, flip)})
            else:
                ret[ex] = ret_send[0]

    gather_rows(0)
    row_gathers[0].forward()
    gather_rows(1)
    row_gathers[1].forward()
    activate(0)
    gather_rows(2)
    row_gathers[2].forward()
    hid_gathers[0].forward()
    activate(1)
    finish_rows(0)
    gather_rows(3)
    row_gathers[3].forward()
    hid_gathers[1].forward()
    activate(2)
    finish_rows(1)
    hid_gathers[2].forward()
    activate(3)
    finish_rows(2)
    hid_gathers[3].forward()

    for i in range(1, PLANES):
        arrive(info.at[peer[i]], info_base + peer[i])
    e_row, e_col = iota((128, 512), 0), iota((128, 512), 1)
    pick = onehot(e_row == (e_col >> 4))
    chosen = dot(info[:, 0].reshape(128, 128).astype(BF), pick)
    meets = (chosen == (e_col & 1).astype(F32)) & ((e_row >> 4) == ((e_col >> 1) & 7))
    mixing = [
        jnp.where(meets, dot(part, pick), 0.0).astype(BF)
        for part in thirds(info[:, 1].reshape(128, 128))
    ]

    finish_rows(3)
    for n, (d, flip) in enumerate(slots):
        if n > 0:
            arrive(ret.at[exp_at(d, flip)], ret_base + n)
    returned = ret[...].reshape(512, WIDE)
    added = dot(mixing[0], returned) + dot(mixing[1], returned) + dot(mixing[2], returned)
    fin_send[...] = added.astype(BF).reshape(PLANES, TOK, WIDE)
    fin_base = take("recv", PLANES)
    for i in YS + (1, 3, 7, 5):
        send(fin_send.at[peer[i]], fin.at[p], fin_base + p, plane(i))
    fin[p] = fin_send[p]
    for i in range(1, PLANES):
        arrive(fin.at[peer[i]], fin_base + peer[i])
    for j in range(PLANES):
        total = stream_buf[j].astype(F32) + fin[j].astype(F32)
        out_ref[:, j * WIDE : (j + 1) * WIDE] = total.astype(BF)
    for copy in started:
        copy.wait_send()


def local(
    resid,
    query,
    key_new,
    value_new,
    cache_key,
    cache_value,
    cache_len,
    block_of,
    out_proj,
    norm_gain,
    routes,
    route_logits,
    w_gate,
    w_up,
    w_down,
):
    rates = np.exp(np.arange(HD // 2, dtype=np.float64) * (-2.0 * math.log(1000000.0) / HD))
    rates = jnp.asarray(np.concatenate([rates, rates])[None, :].astype(np.float32))
    smem = pl.BlockSpec(memory_space=pltpu.SMEM)
    vmem = pl.BlockSpec(memory_space=pltpu.VMEM)
    hbm = pl.BlockSpec(memory_space=pl.ANY)
    q_rows = 2 * GROUP * TOK
    scratch = [
        pltpu.VMEM((q_rows, HD), BF),
        pltpu.VMEM((GROUP * TOK, HD), BF),
        pltpu.VMEM((PLANES, 2, 2, KEYS, HD), BF),
        pltpu.VMEM((2, KEYS, HD), BF),
        pltpu.VMEM((PLANES + 1, q_rows, 256), F32),
        pltpu.VMEM((q_rows, 128), F32),
        pltpu.VMEM((2, PLANES, TOK, 2048), BF),
        pltpu.VMEM((2, 2048, 256), BF),
        pltpu.VMEM((2, PLANES * TOK, 256), F32),
        pltpu.VMEM((2, PLANES * TOK, 256), F32),
        pltpu.VMEM((PLANES, TOK, WIDE), BF),
        pltpu.VMEM((PLANES, TOK, WIDE), BF),
        pltpu.VMEM((PLANES, TOK, WIDE), BF),
        pltpu.VMEM((PLANES, 2, TOK, 128), F32),
        pltpu.VMEM((NEXP, 16, WIDE), BF),
        pltpu.VMEM((NEXP, 16, WIDE), BF),
        pltpu.VMEM((CHUNKS, PLANES, PLANES, 16, WIDE), BF),
        pltpu.VMEM((256, 4096), BF),
        pltpu.VMEM((256, 4096), BF),
        pltpu.VMEM((2, PLANES, 256, 256), BF),
        pltpu.VMEM((CHUNKS, PLANES, 192, 128), BF),
        pltpu.VMEM((NEXP, 16, WIDE), BF),
        pltpu.VMEM((NEXP, 16, WIDE), BF),
        pltpu.VMEM((PLANES, TOK, WIDE), BF),
        pltpu.VMEM((PLANES, TOK, WIDE), BF),
        pltpu.SemaphoreType.DMA((SENDS,)),
        pltpu.SemaphoreType.DMA((RECVS,)),
        pltpu.SemaphoreType.DMA((8,)),
    ]
    out = pl.pallas_call(
        kernel,
        out_shape=jax.ShapeDtypeStruct((TOK, 4096), BF),
        in_specs=[smem, smem] + [vmem] * 10 + [hbm] * 4,
        out_specs=vmem,
        scratch_shapes=scratch,
        compiler_params=pltpu.CompilerParams(
            collective_id=0, has_side_effects=True, vmem_limit_bytes=56 * 2**20
        ),
        name="layer",
    )(
        cache_len,
        block_of,
        rates,
        resid[0],
        query[0],
        key_new[0],
        value_new[0],
        cache_key[0],
        cache_value[0],
        norm_gain[None, :],
        routes[0],
        route_logits[0],
        out_proj,
        w_gate[0],
        w_up[0],
        w_down[0].reshape(PLANES, 192, 256),
    )
    return out[None]


def solution(mesh):
    rows = P("exp", "ctx", None)
    in_specs = (
        rows,
        rows,
        rows,
        rows,
        rows,
        rows,
        P("exp"),
        P(),
        P(None, "ctx"),
        P(),
        rows,
        rows,
        rows,
        rows,
        P("exp", None, "ctx"),
    )
    return jax.shard_map(local, mesh=mesh, in_specs=in_specs, out_specs=rows, check_vma=False)
```

```python
import math

import jax
import jax.numpy as jnp
import numpy as np
from jax import lax
from jax.experimental import pallas as pl
from jax.experimental.pallas import tpu as pltpu
from jax.sharding import PartitionSpec as P

MESH = pl.DeviceIdType.MESH
BF = jnp.bfloat16
F32 = jnp.float32
HD = 128
TOK = 16
CACHED = 128
KEYS = TOK + CACHED
GROUP = 16
PLANES = 8
WIDE = 512
NEXP = 32
UNITS = 96
OFFSETS = ((0, 1, -1, 2), (6, 5, -5, -4), (8, 7, -7, -6), (4, 3, -3, -2))
CHUNKS = len(OFFSETS)
PER = 8
ROWS = PER * 2 * PLANES
YS = (2, 6, 4)
NEG = -1e30
SENDS = 304
RECVS = 336


def iota(shape, axis):
    return lax.broadcasted_iota(jnp.int32, shape, axis)


def onehot(condition):
    return jnp.where(condition, 1.0, 0.0).astype(BF)


def dot(a, b):
    return jnp.dot(a, b, preferred_element_type=F32)


def dot_t(a, b):
    return lax.dot_general(a, b, (((1,), (1,)), ((), ())), preferred_element_type=F32)


def thirds(x):
    high = x.astype(BF)
    rest = x - high.astype(F32)
    middle = rest.astype(BF)
    return high, middle, (rest - middle.astype(F32)).astype(BF)


def kernel(
    length_hbm,
    block_hbm,
    rates_hbm,
    query_hbm,
    key_new_hbm,
    value_new_hbm,
    cache_key_hbm,
    cache_value_hbm,
    resid_hbm,
    gain_hbm,
    routes_hbm,
    logits_hbm,
    out_proj_hbm,
    gate_hbm,
    up_hbm,
    down_hbm,
    out_ref,
    length_ref,
    block_ref,
    rates_ref,
    query_ref,
    key_new_ref,
    value_new_ref,
    cache_key_ref,
    cache_value_ref,
    resid_ref,
    gain_ref,
    routes_ref,
    logits_ref,
    q_buf,
    q_stage,
    kv,
    kv_stage,
    score_buf,
    peak_buf,
    mix,
    mix_stage,
    w_out,
    proj_send,
    attn,
    stream_buf,
    info,
    z_send,
    z_recv,
    rows_buf,
    w_gate,
    w_up,
    w_down,
    hid,
    ret_send,
    ret,
    fin_send,
    fin,
    send_sems,
    recv_sems,
    local_sems,
):
    ctx = lax.axis_index("ctx")
    ex = lax.axis_index("exp")
    core, p = lax.rem(ctx, 2), lax.div(ctx, 2)
    y, h = lax.div(p, 2), lax.rem(p, 2)
    z, low = lax.div(ex, 2), lax.rem(ex, 2)
    other = 1 - core
    ys = {0: y, 2: y + 1 - 2 * lax.rem(y, 2), 4: lax.rem(y + 2, 4), 6: 3 - y}
    peer = [2 * ys[i & 6] + ((1 - h) if i & 1 else h) for i in range(PLANES)]
    partner = {"ctx": 2 * p + other}

    def plane(i):
        return {"ctx": 2 * peer[i] + core}

    slots = []
    for chunk in OFFSETS:
        for d in chunk:
            for flip in (0, 1):
                slots.append((d, flip))

    def exp_at(d, flip):
        return 2 * lax.rem(z + d + 16, 16) + (1 - low if flip else low)

    started = []
    counts = {"send": 0, "recv": 0, "local": 0}

    def take(kind, n):
        first = counts[kind]
        counts[kind] += n
        assert counts[kind] <= {"send": SENDS, "recv": RECVS, "local": 16}[kind]
        return first

    def send(src, dst, recv, device):
        copy = pltpu.make_async_remote_copy(
            src_ref=src,
            dst_ref=dst,
            send_sem=send_sems.at[take("send", 1)],
            recv_sem=recv_sems.at[recv],
            device_id=device,
            device_id_type=MESH,
        )
        copy.start()
        started.append(copy)

    def arrive(dst, recv):
        pltpu.make_async_remote_copy(
            src_ref=dst,
            dst_ref=dst,
            send_sem=send_sems.at[0],
            recv_sem=recv_sems.at[recv],
            device_id=partner,
            device_id_type=MESH,
        ).wait_recv()

    class Gather:
        def __init__(self, at):
            self.at = at
            self.base = take("recv", 2 * PLANES)

        def put(self, source, half, i):
            ref = self.at(source, half)
            send(ref, ref, self.base + 2 * source + half, plane(i))

        def wait(self, i, half):
            arrive(self.at(peer[i], half), self.base + 2 * peer[i] + half)

        def start(self):
            self.put(p, 0, 1)

        def spread(self, half):
            for i in YS:
                self.put(p, half, i)

        def rest(self):
            for half in (1, 0):
                for i in YS:
                    self.put(p, half, i)
            self.put(p, 1, 1)

        def forward(self):
            self.wait(1, 0)
            for i in YS:
                self.put(peer[1], 0, i)
            for i in YS:
                self.wait(i, 1)
                self.put(peer[i], 1, 1)

        def finish(self):
            for i in YS:
                self.wait(i, 0)
            self.wait(1, 1)
            for i in YS:
                self.wait(i + 1, 0)
                self.wait(i + 1, 1)

    barrier = pltpu.get_barrier_semaphore()
    pl.semaphore_signal(barrier, inc=1, device_id=partner, device_id_type=MESH)
    for i in range(1, PLANES):
        pl.semaphore_signal(barrier, inc=1, device_id=plane(i), device_id_type=MESH)
    for d, flip in slots[1:]:
        pl.semaphore_signal(
            barrier, inc=1, device_id={"exp": exp_at(d, flip)}, device_id_type=MESH
        )

    loads = []
    for src, dst in (
        (length_hbm, length_ref),
        (block_hbm, block_ref),
        (cache_key_hbm, cache_key_ref),
        (cache_value_hbm, cache_value_ref),
        (rates_hbm, rates_ref),
        (key_new_hbm, key_new_ref),
        (value_new_hbm, value_new_ref),
        (query_hbm, query_ref),
        (routes_hbm, routes_ref),
        (logits_hbm, logits_ref),
        (resid_hbm, resid_ref),
        (gain_hbm, gain_ref),
    ):
        copy = pltpu.make_async_copy(src, dst, local_sems.at[take("local", 1)])
        copy.start()
        loads.append(copy)
    mine96 = pl.ds(pl.multiple_of(core * UNITS, 16), UNITS)
    head192 = pl.ds(0, 2 * UNITS)
    locals_ = []
    for src, dst in (
        (out_proj_hbm, w_out.at[core]),
        (gate_hbm, w_gate.at[mine96]),
        (up_hbm, w_up.at[mine96]),
        (down_hbm, w_down.at[core, :, head192]),
    ):
        copy = pltpu.make_async_copy(src, dst, local_sems.at[take("local", 1)])
        copy.start()
        locals_.append(copy)

    first = core == 0
    for copy in loads[:2]:
        copy.wait()
    length = length_ref[0]
    block_mine = block_ref[ctx]
    block_other = block_ref[2 * p + other]
    position = (iota((TOK, HD), 0) + (length + block_mine * TOK)).astype(F32)

    def rope(v):
        v = v.astype(F32)
        return (v * cosine + pltpu.roll(v, HD // 2, 1) * sine).astype(BF)

    for copy in loads[2:10]:
        copy.wait()
    angles = position * rates_ref[...]
    cosine = jnp.cos(angles)
    sine = jnp.where(iota((TOK, HD), 1) < HD // 2, -1.0, 1.0) * jnp.sin(angles)
    for g in range(GROUP):
        low_head = rope(query_ref[:, g * HD : (g + 1) * HD])
        high_head = rope(query_ref[:, (GROUP + g) * HD : (GROUP + g + 1) * HD])
        q_buf[g * TOK : (g + 1) * TOK] = jnp.where(first, low_head, high_head)
        q_stage[g * TOK : (g + 1) * TOK] = jnp.where(first, high_head, low_head)
    for which, cached_ref, new_ref in ((0, cache_key_ref, key_new_ref), (1, cache_value_ref, value_new_ref)):
        old = [cached_ref[:, n * HD : (n + 1) * HD] for n in (0, 1)]
        new = [new_ref[:, n * HD : (n + 1) * HD] for n in (0, 1)]
        if which == 0:
            new = [rope(v) for v in new]
        kv[p, 0, which, :CACHED] = jnp.where(first, old[0], old[1])
        kv[p, 0, which, CACHED:] = jnp.where(first, new[0], new[1])
        kv_stage[which, :CACHED] = jnp.where(first, old[1], old[0])
        kv_stage[which, CACHED:] = jnp.where(first, new[1], new[0])

    logits = logits_ref[...]
    powers = jnp.exp(logits - jnp.max(logits, axis=0, keepdims=True))
    shares = powers / jnp.sum(powers, axis=0, keepdims=True)
    routes = jnp.concatenate([routes_ref[...], jnp.full((8, 128 - TOK), -1, jnp.int32)], axis=1)
    shares = jnp.concatenate([shares, jnp.zeros((8, 128 - TOK), F32)], axis=1)
    expert = iota((NEXP, 128), 0)
    token = iota((NEXP, 128), 1)
    taken = jnp.zeros((NEXP, 128), F32)
    share = jnp.zeros((NEXP, 128), F32)
    for x in range(8):
        hit = routes[x : x + 1] == expert
        taken = jnp.where(hit, 1.0, taken)
        share = share + jnp.where(hit, shares[x : x + 1], 0.0)
    rank = taken
    for step in (1, 2, 4, 8):
        rank = rank + jnp.where(token >= step, pltpu.roll(rank, step, 1), 0.0)
    row_of = jnp.where(taken > 0.0, rank - 1.0, -1.0)
    rest = jnp.zeros((128 - NEXP, 128), F32)
    row_of = jnp.concatenate([row_of, rest], axis=0).T[:TOK]
    share = jnp.concatenate([share, rest], axis=0).T[:TOK]
    info[p, 0] = row_of
    info[p, 1] = share

    pl.semaphore_wait(barrier, PLANES + len(slots) - 1)

    kv_gather = Gather(lambda source, half: kv.at[source, half])
    pair_kv, pair_q = take("recv", 1), take("recv", 1)
    send(kv_stage, kv.at[p, 1], pair_kv, partner)
    kv_gather.start()
    q_theirs = q_buf.at[pl.ds(GROUP * TOK, GROUP * TOK)]
    send(q_stage, q_theirs, pair_q, partner)
    arrive(kv.at[p, 1], pair_kv)
    kv_gather.rest()
    pair_weights = [take("recv", 1) for _ in range(4)]
    send(out_proj_hbm, w_out.at[core], pair_weights[0], partner)
    send(gate_hbm, w_gate.at[mine96], pair_weights[1], partner)
    send(up_hbm, w_up.at[mine96], pair_weights[2], partner)
    send(down_hbm, w_down.at[core, :, head192], pair_weights[3], partner)
    info_base = take("recv", PLANES)
    for i in range(1, PLANES):
        send(info.at[p], info.at[p], info_base + p, plane(i))

    row8 = jnp.concatenate([row_of.astype(BF)] * PLANES, axis=0)
    s_row, s_lane = iota((512, 128), 0), iota((512, 128), 1)
    spread = dot_t(onehot((s_row >> 4) == s_lane), row8)
    select = onehot(
        (spread == ((s_row >> 3) & 1).astype(F32)) & ((s_row & 7) == (s_lane >> 4))
    )

    scale = HD ** (-0.5)
    arrive(q_theirs, pair_q)
    q_rows = 2 * GROUP * TOK
    QB = 128

    key_lane = iota((1, 256), 1)

    def score(slot, keys, visible_of):
        def step(rb, carry):
            rows = pl.ds(pl.multiple_of(rb * QB, QB), QB)
            s = dot_t(q_buf[rows], keys) * scale
            s = jnp.where(visible_of(rb), s, NEG)
            score_buf[slot, rows] = s
            top = jnp.maximum(s[:, :128], s[:, 128:])
            peak_buf[rows] = jnp.maximum(peak_buf[rows], top)
            return carry

        lax.fori_loop(0, q_rows // QB, step, 0)

    def score_cached(i):
        source = peer[i]
        keys = jnp.concatenate([kv[source, 0, 0, :CACHED], kv[source, 1, 0, :CACHED]], axis=0)
        near = (2 * source + core) * CACHED
        far = (2 * source + other) * CACHED
        slot = jnp.where(key_lane < CACHED, near + key_lane, far + key_lane - CACHED)
        visible = slot < length
        score(source, keys, lambda rb: visible)

    peak_buf[...] = jnp.full((q_rows, 128), NEG, F32)
    score_cached(0)
    kv_gather.forward()
    for i in YS:
        kv_gather.wait(i, 0)
        score_cached(i)
    kv_gather.wait(1, 1)
    score_cached(1)
    for i in (3, 7, 5):
        kv_gather.wait(i, 0)
        kv_gather.wait(i, 1)
        score_cached(i)
    new_keys = jnp.concatenate(
        [kv[s, o, 0, CACHED:] for s in range(PLANES) for o in (0, 1)], axis=0
    )
    new_values = jnp.concatenate(
        [kv[s, o, 1, CACHED:] for s in range(PLANES) for o in (0, 1)], axis=0
    )
    key_offset = jnp.zeros((1, 256), jnp.int32)
    for s in range(PLANES):
        for o in (0, 1):
            block = block_ref[2 * s + (core if o == 0 else other)]
            key_offset = jnp.where((key_lane >> 4) == 2 * s + o, block * TOK, key_offset)
    key_offset = key_offset + (key_lane & 15)

    def causal(rb):
        block = jnp.where(rb < 2, block_mine, block_other)
        return key_offset <= (iota((QB, 256), 0) & 15) + block * TOK

    score(PLANES, new_keys, causal)

    def weigh(rb, carry):
        rows = pl.ds(pl.multiple_of(rb * QB, QB), QB)
        peak = jnp.max(peak_buf[rows], axis=1, keepdims=True)
        total = jnp.zeros((QB, 128), F32)
        mixed = jnp.zeros((QB, HD), F32)
        for s in range(PLANES + 1):
            weights = jnp.exp(score_buf[s, rows] - peak)
            total = total + weights[:, :128] + weights[:, 128:]
            if s < PLANES:
                values = jnp.concatenate([kv[s, 0, 1, :CACHED], kv[s, 1, 1, :CACHED]], axis=0)
            else:
                values = new_values
            mixed = mixed + dot(weights.astype(BF), values)
        mixed = (mixed / jnp.sum(total, axis=1, keepdims=True)).astype(BF)
        q_buf[rows] = mixed
        return carry

    def mix_half(o, ref):
        lax.fori_loop(2 * o, 2 * o + 2, weigh, 0)
        for g in range(GROUP):
            r = (o * GROUP + g) * TOK
            ref[:, g * HD : (g + 1) * HD] = q_buf[r : r + TOK]

    pair_mix = take("recv", 1)
    mix_gather = Gather(lambda source, half: mix.at[half, source])
    mix_half(1, mix_stage)
    send(mix_stage, mix.at[1, p], pair_mix, partner)
    mix_half(0, mix.at[0, p])
    mix_gather.start()
    arrive(mix.at[1, p], pair_mix)
    mix_gather.rest()
    mix_gather.forward()
    locals_[0].wait()
    arrive(w_out.at[other], pair_weights[0])
    for i in YS + (3, 7, 5):
        mix_gather.wait(i, 0)
    left = mix[0].reshape(PLANES * TOK, 2048)
    projected = [dot(left, w_out[o, core]) for o in (0, 1)]
    for i in (1, 3, 7, 5):
        mix_gather.wait(i, 1)
    left = mix[1].reshape(PLANES * TOK, 2048)
    for o in (0, 1):
        block = projected[o] + dot(left, w_out[o, other])
        proj_send[:, :, o * 256 : (o + 1) * 256] = block.astype(BF).reshape(PLANES, TOK, 256)
    attn_base = take("recv", PLANES)
    for i in YS + (1, 3, 7, 5):
        send(proj_send.at[peer[i]], attn.at[p], attn_base + p, plane(i))
    attn[p] = proj_send[p]
    for i in range(1, PLANES):
        arrive(attn.at[peer[i]], attn_base + peer[i])

    for copy in loads[10:]:
        copy.wait()
    square = jnp.zeros((TOK, 1), F32)
    streams = []
    for j in range(PLANES):
        cols = slice(j * WIDE, (j + 1) * WIDE)
        v = (resid_ref[:, cols].astype(F32) + attn[j].astype(F32)).astype(BF)
        stream_buf[j] = v
        v = v.astype(F32)
        streams.append(v)
        square = square + jnp.sum(v * v, axis=1, keepdims=True)
    inverse = lax.rsqrt(square * (1.0 / (PLANES * WIDE)) + 1e-06)
    normed = jnp.concatenate(
        [
            (streams[j] * inverse * gain_ref[:, j * WIDE : (j + 1) * WIDE]).astype(BF)
            for j in range(PLANES)
        ],
        axis=0,
    )
    z_send[...] = dot(select, normed).astype(BF).reshape(NEXP, 16, WIDE)

    z_base = take("recv", len(slots))
    z_recv[0] = z_send[ex]
    for n, (d, flip) in enumerate(slots):
        if n > 0:
            to = exp_at(d, flip)
            send(z_send.at[to], z_recv.at[n], z_base + n, {"exp": to})

    for copy in locals_[1:]:
        copy.wait()
    theirs96 = pl.ds(pl.multiple_of(other * UNITS, 16), UNITS)
    arrive(w_gate.at[theirs96], pair_weights[1])
    arrive(w_up.at[theirs96], pair_weights[2])
    arrive(w_down.at[other, :, head192], pair_weights[3])
    w_gate[192:] = w_gate[128:192]
    w_up[192:] = w_up[128:192]
    for o in (0, 1):
        w_down[o, :, 192:] = w_down[o, :, 128:192]

    r_, c_ = iota((128, 128), 0), iota((128, 128), 1)
    to_blocks = onehot(((r_ >> 4) == (c_ & 7)) & ((r_ & 15) == (c_ >> 3)))
    to_requests = onehot(
        ((r_ >> 4) == ((c_ >> 1) & 7)) & (((r_ >> 1) & 7) == (c_ >> 4)) & ((r_ & 1) == (c_ & 1))
    )
    ret_base = take("recv", len(slots))
    row_gathers = [
        Gather(lambda source, half, q=q: rows_buf.at[q, source, pl.ds(4 * half, 4)])
        for q in range(CHUNKS)
    ]
    hid_gathers = [
        Gather(lambda source, half, q=q: hid.at[q, source, pl.ds(UNITS * half, UNITS)])
        for q in range(CHUNKS)
    ]

    def gather_rows(q):
        for n in range(q * PER, (q + 1) * PER):
            if n > 0:
                arrive(z_recv.at[n], z_base + n)
        block = z_recv[q * PER : (q + 1) * PER].reshape(128, WIDE)
        rows_buf[q, p] = dot(to_blocks, block).astype(BF).reshape(PLANES, 16, WIDE)
        row_gathers[q].start()
        row_gathers[q].rest()

    def activate(q):
        row_gathers[q].finish()
        gate = jnp.zeros((ROWS, 256), F32)
        upward = jnp.zeros((ROWS, 256), F32)
        for j in range(PLANES):
            rows = rows_buf[q, :, j].reshape(ROWS, WIDE)
            cols = slice(j * WIDE, (j + 1) * WIDE)
            gate = gate + dot_t(rows, w_gate[:, cols])
            upward = upward + dot_t(rows, w_up[:, cols])
        hidden = (gate / (1.0 + jnp.exp(-gate)) * upward).astype(BF)
        tail = hidden[:, 128:]
        left = iota((64, 128), 1) < 64
        hid[q, p, :128] = hidden[:, :128]
        hid[q, p, 128:] = jnp.where(left, tail[:64], tail[64:])
        hid_gathers[q].start()
        hid_gathers[q].spread(0)
        hid_gathers[q].spread(1)
        hid_gathers[q].put(p, 1, 1)

    def finish_rows(q):
        hid_gathers[q].finish()
        left = iota((64, 128), 1) < 64
        result = [jnp.zeros((ROWS, 256), F32) for _ in (0, 1)]
        zero = jnp.zeros((64, 128), BF)
        for s in range(PLANES):
            tail = hid[q, s, 128:]
            tail = jnp.concatenate(
                [jnp.where(left, tail, zero), jnp.where(left, zero, tail)], axis=0
            )
            hidden = jnp.concatenate([hid[q, s, :128], tail], axis=1)
            for o in (0, 1):
                result[o] = result[o] + dot(hidden, w_down[o, s])
        for o in (0, 1):
            block = dot(to_requests, result[o].astype(BF)).astype(BF).reshape(PER, 16, 256)
            ret_send[q * PER : (q + 1) * PER, :, o * 256 : (o + 1) * 256] = block
        for n in range(q * PER, (q + 1) * PER):
            d, flip = slots[n]
            if n > 0:
                send(ret_send.at[n], ret.at[ex], ret_base + n, {"exp": exp_at(-d, flip)})
            else:
                ret[ex] = ret_send[0]

    gather_rows(0)
    row_gathers[0].forward()
    gather_rows(1)
    activate(0)
    row_gathers[1].forward()
    hid_gathers[0].forward()
    gather_rows(2)
    activate(1)
    finish_rows(0)
    row_gathers[2].forward()
    hid_gathers[1].forward()
    gather_rows(3)
    activate(2)
    finish_rows(1)
    row_gathers[3].forward()
    hid_gathers[2].forward()
    activate(3)
    finish_rows(2)
    hid_gathers[3].forward()

    for i in range(1, PLANES):
        arrive(info.at[peer[i]], info_base + peer[i])
    e_row, e_col = iota((128, 512), 0), iota((128, 512), 1)
    pick = onehot(e_row == (e_col >> 4))
    chosen = dot(info[:, 0].reshape(128, 128).astype(BF), pick)
    meets = (chosen == (e_col & 1).astype(F32)) & ((e_row >> 4) == ((e_col >> 1) & 7))
    mixing = [
        jnp.where(meets, dot(part, pick), 0.0).astype(BF)
        for part in thirds(info[:, 1].reshape(128, 128))
    ]

    finish_rows(3)
    for copy in started:
        copy.wait_send()
    started.clear()
    for n, (d, flip) in enumerate(slots):
        if n > 0:
            arrive(ret.at[exp_at(d, flip)], ret_base + n)
    returned = ret[...].reshape(512, WIDE)
    added = dot(mixing[0], returned) + dot(mixing[1], returned) + dot(mixing[2], returned)
    fin_send[...] = added.astype(BF).reshape(PLANES, TOK, WIDE)
    fin_base = take("recv", PLANES)
    for i in YS + (1, 3, 7, 5):
        send(fin_send.at[peer[i]], fin.at[p], fin_base + p, plane(i))
    fin[p] = fin_send[p]
    for i in range(1, PLANES):
        arrive(fin.at[peer[i]], fin_base + peer[i])
    for j in range(PLANES):
        total = stream_buf[j].astype(F32) + fin[j].astype(F32)
        out_ref[:, j * WIDE : (j + 1) * WIDE] = total.astype(BF)
    for copy in started:
        copy.wait_send()


def local(
    resid,
    query,
    key_new,
    value_new,
    cache_key,
    cache_value,
    cache_len,
    block_of,
    out_proj,
    norm_gain,
    routes,
    route_logits,
    w_gate,
    w_up,
    w_down,
):
    rates = np.exp(np.arange(HD // 2, dtype=np.float64) * (-2.0 * math.log(1000000.0) / HD))
    rates = jnp.asarray(np.concatenate([rates, rates])[None, :].astype(np.float32))
    vmem = pl.BlockSpec(memory_space=pltpu.VMEM)
    hbm = pl.BlockSpec(memory_space=pl.ANY)
    q_rows = 2 * GROUP * TOK
    scratch = [
        pltpu.SMEM((1,), jnp.int32),
        pltpu.SMEM((16,), jnp.int32),
        pltpu.VMEM((1, HD), F32),
        pltpu.VMEM((TOK, 4096), BF),
        pltpu.VMEM((TOK, 256), BF),
        pltpu.VMEM((TOK, 256), BF),
        pltpu.VMEM((CACHED, 256), BF),
        pltpu.VMEM((CACHED, 256), BF),
        pltpu.VMEM((TOK, 4096), BF),
        pltpu.VMEM((1, 4096), F32),
        pltpu.VMEM((8, TOK), jnp.int32),
        pltpu.VMEM((8, TOK), F32),
        pltpu.VMEM((q_rows, HD), BF),
        pltpu.VMEM((GROUP * TOK, HD), BF),
        pltpu.VMEM((PLANES, 2, 2, KEYS, HD), BF),
        pltpu.VMEM((2, KEYS, HD), BF),
        pltpu.VMEM((PLANES + 1, q_rows, 256), F32),
        pltpu.VMEM((q_rows, 128), F32),
        pltpu.VMEM((2, PLANES, TOK, 2048), BF),
        pltpu.VMEM((TOK, 2048), BF),
        pltpu.VMEM((2, 2, 2048, 256), BF),
        pltpu.VMEM((PLANES, TOK, WIDE), BF),
        pltpu.VMEM((PLANES, TOK, WIDE), BF),
        pltpu.VMEM((PLANES, TOK, WIDE), BF),
        pltpu.VMEM((PLANES, 2, TOK, 128), F32),
        pltpu.VMEM((NEXP, 16, WIDE), BF),
        pltpu.VMEM((NEXP, 16, WIDE), BF),
        pltpu.VMEM((CHUNKS, PLANES, PLANES, 16, WIDE), BF),
        pltpu.VMEM((256, 4096), BF),
        pltpu.VMEM((256, 4096), BF),
        pltpu.VMEM((2, PLANES, 256, 256), BF),
        pltpu.VMEM((CHUNKS, PLANES, 192, 128), BF),
        pltpu.VMEM((NEXP, 16, WIDE), BF),
        pltpu.VMEM((NEXP, 16, WIDE), BF),
        pltpu.VMEM((PLANES, TOK, WIDE), BF),
        pltpu.VMEM((PLANES, TOK, WIDE), BF),
        pltpu.SemaphoreType.DMA((SENDS,)),
        pltpu.SemaphoreType.DMA((RECVS,)),
        pltpu.SemaphoreType.DMA((16,)),
    ]
    out = pl.pallas_call(
        kernel,
        out_shape=jax.ShapeDtypeStruct((TOK, 4096), BF),
        in_specs=[hbm] * 16,
        out_specs=vmem,
        scratch_shapes=scratch,
        compiler_params=pltpu.CompilerParams(
            collective_id=0, has_side_effects=True, vmem_limit_bytes=56 * 2**20
        ),
        name="layer",
    )(
        cache_len,
        block_of,
        rates,
        query[0],
        key_new[0],
        value_new[0],
        cache_key[0],
        cache_value[0],
        resid[0],
        norm_gain[None, :],
        routes[0].T,
        route_logits[0].T,
        out_proj.reshape(2, 2048, 256),
        w_gate[0],
        w_up[0],
        w_down[0].reshape(PLANES, 192, 256),
    )
    return out[None]


def solution(mesh):
    rows = P("exp", "ctx", None)
    in_specs = (
        rows,
        rows,
        rows,
        rows,
        rows,
        rows,
        P("exp"),
        P(),
        P(None, "ctx"),
        P(),
        rows,
        rows,
        rows,
        rows,
        P("exp", None, "ctx"),
    )
    return jax.shard_map(local, mesh=mesh, in_specs=in_specs, out_specs=rows, check_vma=False)
```

```python
import math

import jax
import jax.numpy as jnp
import numpy as np
from jax import lax
from jax.experimental import pallas as pl
from jax.experimental.pallas import tpu as pltpu
from jax.sharding import PartitionSpec as P

MESH = pl.DeviceIdType.MESH
BF = jnp.bfloat16
F32 = jnp.float32
HD = 128
TOK = 16
CACHED = 128
KEYS = TOK + CACHED
GROUP = 16
PLANES = 8
WIDE = 512
NEXP = 32
UNITS = 96
OFFSETS = ((0, 1, -1, -2), (6, 5, -5, -4), (8, 7, -7, -6), (4, 3, -3, 2))
CHUNKS = len(OFFSETS)
PER = 8
ROWS = PER * 2 * PLANES
YS = (2, 6, 4)
NEG = -1e30
SENDS = 304
RECVS = 336


def iota(shape, axis):
    return lax.broadcasted_iota(jnp.int32, shape, axis)


def onehot(condition):
    return jnp.where(condition, 1.0, 0.0).astype(BF)


def dot(a, b):
    return jnp.dot(a, b, preferred_element_type=F32)


def dot_t(a, b):
    return lax.dot_general(a, b, (((1,), (1,)), ((), ())), preferred_element_type=F32)


def thirds(x):
    high = x.astype(BF)
    rest = x - high.astype(F32)
    middle = rest.astype(BF)
    return high, middle, (rest - middle.astype(F32)).astype(BF)


def kernel(
    length_hbm,
    block_hbm,
    rates_hbm,
    query_hbm,
    key_new_hbm,
    value_new_hbm,
    cache_key_hbm,
    cache_value_hbm,
    resid_hbm,
    gain_hbm,
    routes_hbm,
    logits_hbm,
    out_proj_hbm,
    gate_hbm,
    up_hbm,
    down_hbm,
    out_ref,
    length_ref,
    block_ref,
    rates_ref,
    query_ref,
    key_new_ref,
    value_new_ref,
    cache_key_ref,
    cache_value_ref,
    resid_ref,
    gain_ref,
    routes_ref,
    logits_ref,
    q_buf,
    q_stage,
    kv,
    kv_stage,
    score_buf,
    peak_buf,
    mix,
    mix_stage,
    w_out,
    proj_send,
    attn,
    stream_buf,
    info,
    z_send,
    z_recv,
    rows_send,
    rows_buf,
    sum_send,
    sum_recv,
    sum_own,
    w_gate,
    w_up,
    w_down,
    hid,
    ret_send,
    ret,
    fin_send,
    fin,
    send_sems,
    recv_sems,
    local_sems,
):
    ctx = lax.axis_index("ctx")
    ex = lax.axis_index("exp")
    core, p = lax.rem(ctx, 2), lax.div(ctx, 2)
    y, h = lax.div(p, 2), lax.rem(p, 2)
    z, low = lax.div(ex, 2), lax.rem(ex, 2)
    other = 1 - core
    ys = {0: y, 2: y + 1 - 2 * lax.rem(y, 2), 4: lax.rem(y + 2, 4), 6: 3 - y}
    peer = [2 * ys[i & 6] + ((1 - h) if i & 1 else h) for i in range(PLANES)]
    partner = {"ctx": 2 * p + other}

    def plane(i):
        return {"ctx": 2 * peer[i] + core}

    slots = []
    for chunk in OFFSETS:
        for d in chunk:
            for flip in (0, 1):
                slots.append((d, flip))

    def exp_at(d, flip):
        return 2 * lax.rem(z + d + 16, 16) + (1 - low if flip else low)

    started = []
    counts = {"send": 0, "recv": 0, "local": 0}

    def take(kind, n):
        first = counts[kind]
        counts[kind] += n
        assert counts[kind] <= {"send": SENDS, "recv": RECVS, "local": 16}[kind]
        return first

    def send(src, dst, recv, device):
        copy = pltpu.make_async_remote_copy(
            src_ref=src,
            dst_ref=dst,
            send_sem=send_sems.at[take("send", 1)],
            recv_sem=recv_sems.at[recv],
            device_id=device,
            device_id_type=MESH,
        )
        copy.start()
        started.append(copy)

    def arrive(dst, recv):
        pltpu.make_async_remote_copy(
            src_ref=dst,
            dst_ref=dst,
            send_sem=send_sems.at[0],
            recv_sem=recv_sems.at[recv],
            device_id=partner,
            device_id_type=MESH,
        ).wait_recv()

    class Gather:
        def __init__(self, at):
            self.at = at
            self.base = take("recv", 2 * PLANES)

        def put(self, source, half, i):
            ref = self.at(source, half)
            send(ref, ref, self.base + 2 * source + half, plane(i))

        def wait(self, i, half):
            arrive(self.at(peer[i], half), self.base + 2 * peer[i] + half)

        def start(self):
            self.put(p, 0, 1)
            for half in (0, 1):
                for i in YS:
                    self.put(p, half, i)
            self.put(p, 1, 1)

        def first(self):
            self.put(p, 0, 1)

        def rest(self):
            for half in (1, 0):
                for i in YS:
                    self.put(p, half, i)
            self.put(p, 1, 1)

        def forward(self):
            self.wait(1, 0)
            for i in YS:
                self.put(peer[1], 0, i)
            for i in YS:
                self.wait(i, 1)
                self.put(peer[i], 1, 1)

        def finish(self):
            for i in YS:
                self.wait(i, 0)
            self.wait(1, 1)
            for i in YS:
                self.wait(i + 1, 0)
                self.wait(i + 1, 1)

    class RowGather:
        def __init__(self, q):
            self.q = q
            self.base = take("recv", PLANES)

        def put(self, i, to):
            ref = rows_buf.at[self.q, peer[i]]
            send(ref, ref, self.base + peer[i], plane(to))

        def wait(self, i):
            arrive(rows_buf.at[self.q, peer[i]], self.base + peer[i])

        def start(self):
            send(rows_send.at[self.q], rows_buf.at[self.q, p], self.base + p, plane(1))
            for i in YS:
                self.put(0, i)

        def forward(self):
            self.wait(1)
            for i in YS:
                self.put(1, i)

        def finish(self):
            for i in YS + (3, 7, 5):
                self.wait(i)

    class Direct:
        def __init__(self, at):
            self.at = at
            self.base = take("recv", PLANES)

        def start(self):
            for i in YS + (1, 3, 7, 5):
                send(self.at(p), self.at(p), self.base + p, plane(i))

        def forward(self):
            pass

        def finish(self):
            for i in YS + (1, 3, 7, 5):
                arrive(self.at(peer[i]), self.base + peer[i])

    barrier = pltpu.get_barrier_semaphore()
    pl.semaphore_signal(barrier, inc=1, device_id=partner, device_id_type=MESH)
    for i in range(1, PLANES):
        pl.semaphore_signal(barrier, inc=1, device_id=plane(i), device_id_type=MESH)
    for d, flip in slots[1:]:
        pl.semaphore_signal(
            barrier, inc=1, device_id={"exp": exp_at(d, flip)}, device_id_type=MESH
        )

    loads = []
    for src, dst in (
        (length_hbm, length_ref),
        (block_hbm, block_ref),
        (cache_key_hbm, cache_key_ref),
        (cache_value_hbm, cache_value_ref),
        (rates_hbm, rates_ref),
        (key_new_hbm, key_new_ref),
        (value_new_hbm, value_new_ref),
        (query_hbm, query_ref),
        (routes_hbm, routes_ref),
        (logits_hbm, logits_ref),
        (resid_hbm, resid_ref),
        (gain_hbm, gain_ref),
    ):
        copy = pltpu.make_async_copy(src, dst, local_sems.at[take("local", 1)])
        copy.start()
        loads.append(copy)
    mine96 = pl.ds(pl.multiple_of(core * UNITS, 16), UNITS)
    head192 = pl.ds(0, 2 * UNITS)
    near_cols = pl.ds(pl.multiple_of(h * 2048, 2048), 2048)
    far_cols = pl.ds(pl.multiple_of((1 - h) * 2048, 2048), 2048)
    locals_ = []
    for src, dst in (
        (out_proj_hbm, w_out.at[core]),
        (gate_hbm.at[:, near_cols], w_gate.at[0, mine96]),
        (up_hbm.at[:, near_cols], w_up.at[0, mine96]),
        (down_hbm, w_down.at[core, :, head192]),
    ):
        copy = pltpu.make_async_copy(src, dst, local_sems.at[take("local", 1)])
        copy.start()
        locals_.append(copy)

    first = core == 0
    for copy in loads[:2]:
        copy.wait()
    length = length_ref[0]
    block_mine = block_ref[ctx]
    block_other = block_ref[2 * p + other]
    position = (iota((TOK, HD), 0) + (length + block_mine * TOK)).astype(F32)

    def rope(v):
        v = v.astype(F32)
        return (v * cosine + pltpu.roll(v, HD // 2, 1) * sine).astype(BF)

    for copy in loads[2:10]:
        copy.wait()
    angles = position * rates_ref[...]
    cosine = jnp.cos(angles)
    sine = jnp.where(iota((TOK, HD), 1) < HD // 2, -1.0, 1.0) * jnp.sin(angles)
    for g in range(GROUP):
        low_head = rope(query_ref[:, g * HD : (g + 1) * HD])
        high_head = rope(query_ref[:, (GROUP + g) * HD : (GROUP + g + 1) * HD])
        q_buf[g * TOK : (g + 1) * TOK] = jnp.where(first, low_head, high_head)
        q_stage[g * TOK : (g + 1) * TOK] = jnp.where(first, high_head, low_head)
    for which, cached_ref, new_ref in ((0, cache_key_ref, key_new_ref), (1, cache_value_ref, value_new_ref)):
        old = [cached_ref[:, n * HD : (n + 1) * HD] for n in (0, 1)]
        new = [new_ref[:, n * HD : (n + 1) * HD] for n in (0, 1)]
        if which == 0:
            new = [rope(v) for v in new]
        kv[p, 0, which, :CACHED] = jnp.where(first, old[0], old[1])
        kv[p, 0, which, CACHED:] = jnp.where(first, new[0], new[1])
        kv_stage[which, :CACHED] = jnp.where(first, old[1], old[0])
        kv_stage[which, CACHED:] = jnp.where(first, new[1], new[0])

    logits = logits_ref[...]
    powers = jnp.exp(logits - jnp.max(logits, axis=0, keepdims=True))
    shares = powers / jnp.sum(powers, axis=0, keepdims=True)
    routes = jnp.concatenate([routes_ref[...], jnp.full((8, 128 - TOK), -1, jnp.int32)], axis=1)
    shares = jnp.concatenate([shares, jnp.zeros((8, 128 - TOK), F32)], axis=1)
    expert = iota((NEXP, 128), 0)
    token = iota((NEXP, 128), 1)
    taken = jnp.zeros((NEXP, 128), F32)
    share = jnp.zeros((NEXP, 128), F32)
    for x in range(8):
        hit = routes[x : x + 1] == expert
        taken = jnp.where(hit, 1.0, taken)
        share = share + jnp.where(hit, shares[x : x + 1], 0.0)
    rank = taken
    for step in (1, 2, 4, 8):
        rank = rank + jnp.where(token >= step, pltpu.roll(rank, step, 1), 0.0)
    row_of = jnp.where(taken > 0.0, rank - 1.0, -1.0)
    rest = jnp.zeros((128 - NEXP, 128), F32)
    row_of = jnp.concatenate([row_of, rest], axis=0).T[:TOK]
    share = jnp.concatenate([share, rest], axis=0).T[:TOK]
    info[p, 0] = row_of
    info[p, 1] = share

    pl.semaphore_wait(barrier, PLANES + len(slots) - 1)

    kv_gather = Gather(lambda source, half: kv.at[source, half])
    pair_kv, pair_q = take("recv", 1), take("recv", 1)
    send(kv_stage, kv.at[p, 1], pair_kv, partner)
    kv_gather.first()
    q_theirs = q_buf.at[pl.ds(GROUP * TOK, GROUP * TOK)]
    send(q_stage, q_theirs, pair_q, partner)
    arrive(kv.at[p, 1], pair_kv)
    kv_gather.rest()
    pair_weights = [take("recv", 1) for _ in range(4)]
    send(out_proj_hbm, w_out.at[core], pair_weights[0], partner)
    send(gate_hbm.at[:, near_cols], w_gate.at[0, mine96], pair_weights[1], partner)
    send(up_hbm.at[:, near_cols], w_up.at[0, mine96], pair_weights[2], partner)
    send(down_hbm, w_down.at[core, :, head192], pair_weights[3], partner)
    cross_weights = [take("recv", 1) for _ in range(8)]

    def cross(piece):
        src, dst = ((gate_hbm, w_gate), (up_hbm, w_up))[piece // 2]
        rows = pl.ds(48 * (piece % 2), 48)
        to = pl.ds(pl.multiple_of(core * UNITS + 48 * (piece % 2), 16), 48)
        send(src.at[rows, far_cols], dst.at[1, to], cross_weights[piece], plane(1))

    def crossed(piece, whose):
        dst = (w_gate, w_up)[piece // 2]
        return dst.at[1, pl.ds(pl.multiple_of(whose * UNITS + 48 * (piece % 2), 16), 48)]

    info_base = take("recv", PLANES)
    for i in range(1, PLANES):
        send(info.at[p], info.at[p], info_base + p, plane(i))

    row8 = jnp.concatenate([row_of.astype(BF)] * PLANES, axis=0)
    s_row, s_lane = iota((512, 128), 0), iota((512, 128), 1)
    spread = dot_t(onehot((s_row >> 4) == s_lane), row8)
    select = onehot(
        (spread == ((s_row >> 3) & 1).astype(F32)) & ((s_row & 7) == (s_lane >> 4))
    )

    scale = HD ** (-0.5)
    arrive(q_theirs, pair_q)
    q_rows = 2 * GROUP * TOK
    QB = 128

    key_lane = iota((1, 256), 1)

    def score(slot, keys, visible_of):
        def step(rb, carry):
            rows = pl.ds(pl.multiple_of(rb * QB, QB), QB)
            s = dot_t(q_buf[rows], keys) * scale
            s = jnp.where(visible_of(rb), s, NEG)
            score_buf[slot, rows] = s
            top = jnp.maximum(s[:, :128], s[:, 128:])
            peak_buf[rows] = jnp.maximum(peak_buf[rows], top)
            return carry

        lax.fori_loop(0, q_rows // QB, step, 0)

    def score_cached(i):
        source = peer[i]
        keys = jnp.concatenate([kv[source, 0, 0, :CACHED], kv[source, 1, 0, :CACHED]], axis=0)
        near = (2 * source + core) * CACHED
        far = (2 * source + other) * CACHED
        slot = jnp.where(key_lane < CACHED, near + key_lane, far + key_lane - CACHED)
        visible = slot < length
        score(source, keys, lambda rb: visible)

    peak_buf[...] = jnp.full((q_rows, 128), NEG, F32)
    score_cached(0)
    kv_gather.forward()
    cross(0)
    cross(1)
    for i in YS:
        kv_gather.wait(i, 0)
        score_cached(i)
    kv_gather.wait(1, 1)
    score_cached(1)
    for i in (3, 7, 5):
        kv_gather.wait(i, 0)
        kv_gather.wait(i, 1)
        score_cached(i)
    new_keys = jnp.concatenate(
        [kv[s, o, 0, CACHED:] for s in range(PLANES) for o in (0, 1)], axis=0
    )
    new_values = jnp.concatenate(
        [kv[s, o, 1, CACHED:] for s in range(PLANES) for o in (0, 1)], axis=0
    )
    key_offset = jnp.zeros((1, 256), jnp.int32)
    for s in range(PLANES):
        for o in (0, 1):
            block = block_ref[2 * s + (core if o == 0 else other)]
            key_offset = jnp.where((key_lane >> 4) == 2 * s + o, block * TOK, key_offset)
    key_offset = key_offset + (key_lane & 15)

    def causal(rb):
        block = jnp.where(rb < 2, block_mine, block_other)
        return key_offset <= (iota((QB, 256), 0) & 15) + block * TOK

    score(PLANES, new_keys, causal)

    def weigh(rb, carry):
        rows = pl.ds(pl.multiple_of(rb * QB, QB), QB)
        peak = jnp.max(peak_buf[rows], axis=1, keepdims=True)
        total = jnp.zeros((QB, 128), F32)
        mixed = jnp.zeros((QB, HD), F32)
        for s in range(PLANES + 1):
            weights = jnp.exp(score_buf[s, rows] - peak)
            total = total + weights[:, :128] + weights[:, 128:]
            if s < PLANES:
                values = jnp.concatenate([kv[s, 0, 1, :CACHED], kv[s, 1, 1, :CACHED]], axis=0)
            else:
                values = new_values
            mixed = mixed + dot(weights.astype(BF), values)
        mixed = (mixed / jnp.sum(total, axis=1, keepdims=True)).astype(BF)
        q_buf[rows] = mixed
        return carry

    def mix_half(o, ref):
        lax.fori_loop(2 * o, 2 * o + 2, weigh, 0)
        for g in range(GROUP):
            r = (o * GROUP + g) * TOK
            ref[:, g * HD : (g + 1) * HD] = q_buf[r : r + TOK]

    pair_mix = take("recv", 1)
    mix_gather = Gather(lambda source, half: mix.at[half, source])
    mix_half(1, mix_stage)
    send(mix_stage, mix.at[1, p], pair_mix, partner)
    mix_half(0, mix.at[0, p])
    mix_gather.first()
    arrive(mix.at[1, p], pair_mix)
    mix_gather.rest()
    mix_gather.forward()
    locals_[0].wait()
    arrive(w_out.at[other], pair_weights[0])
    for i in YS + (3, 7, 5):
        mix_gather.wait(i, 0)
    left = mix[0].reshape(PLANES * TOK, 2048)
    projected = [dot(left, w_out[o, core]) for o in (0, 1)]
    for i in (1, 3, 7, 5):
        mix_gather.wait(i, 1)
    left = mix[1].reshape(PLANES * TOK, 2048)
    for o in (0, 1):
        block = projected[o] + dot(left, w_out[o, other])
        proj_send[:, :, o * 256 : (o + 1) * 256] = block.astype(BF).reshape(PLANES, TOK, 256)
    attn_base = take("recv", PLANES)
    for i in YS + (1, 3, 7, 5):
        send(proj_send.at[peer[i]], attn.at[p], attn_base + p, plane(i))
    cross(2)
    attn[p] = proj_send[p]
    for i in range(1, PLANES):
        arrive(attn.at[peer[i]], attn_base + peer[i])

    for copy in loads[10:]:
        copy.wait()
    square = jnp.zeros((TOK, 1), F32)
    streams = []
    for j in range(PLANES):
        cols = slice(j * WIDE, (j + 1) * WIDE)
        v = (resid_ref[:, cols].astype(F32) + attn[j].astype(F32)).astype(BF)
        stream_buf[j] = v
        v = v.astype(F32)
        streams.append(v)
        square = square + jnp.sum(v * v, axis=1, keepdims=True)
    inverse = lax.rsqrt(square * (1.0 / (PLANES * WIDE)) + 1e-06)
    normed = jnp.concatenate(
        [
            (streams[j] * inverse * gain_ref[:, j * WIDE : (j + 1) * WIDE]).astype(BF)
            for j in range(PLANES)
        ],
        axis=0,
    )
    z_send[...] = dot(select, normed).astype(BF).reshape(NEXP, 16, WIDE)

    z_base = take("recv", len(slots))
    z_recv[0] = z_send[ex]
    for n, (d, flip) in enumerate(slots):
        if n > 0:
            to = exp_at(d, flip)
            send(z_send.at[to], z_recv.at[n], z_base + n, {"exp": to})
        if n == PER - 1:
            cross(3)

    theirs96 = pl.ds(pl.multiple_of(other * UNITS, 16), UNITS)

    def pass_weights(pieces):
        for piece in pieces:
            ref = crossed(piece, core)
            arrive(ref, cross_weights[piece])
            send(ref, ref, cross_weights[4 + piece], partner)

    def complete_weights():
        for copy in locals_[1:]:
            copy.wait()
        arrive(w_gate.at[0, theirs96], pair_weights[1])
        arrive(w_up.at[0, theirs96], pair_weights[2])
        arrive(w_down.at[other, :, head192], pair_weights[3])
        for piece in range(4):
            arrive(crossed(piece, other), cross_weights[4 + piece])
        for side in (0, 1):
            w_gate[side, 192:] = w_gate[side, 128:192]
            w_up[side, 192:] = w_up[side, 128:192]
        for o in (0, 1):
            w_down[o, :, 192:] = w_down[o, :, 128:192]

    r_, c_ = iota((128, 128), 0), iota((128, 128), 1)
    to_blocks = onehot(((((r_ >> 4) + 4 * h) & 7) == (c_ & 7)) & ((r_ & 15) == (c_ >> 3)))
    to_requests = onehot(
        ((r_ >> 4) == ((c_ >> 1) & 7)) & (((r_ >> 1) & 7) == (c_ >> 4)) & ((r_ & 1) == (c_ & 1))
    )
    ret_base = take("recv", len(slots))
    row_gathers = [RowGather(q) for q in range(CHUNKS)]
    cross_sums = [take("recv", 1) for _ in range(CHUNKS)]
    hid_gathers = [
        Gather(lambda source, half, q=q: hid.at[q, source, pl.ds(UNITS * half, UNITS)])
        for q in range(CHUNKS - 1)
    ]
    hid_gathers.append(Direct(lambda source: hid.at[CHUNKS - 1, source]))

    def gather_rows(q):
        for n in range(q * PER, (q + 1) * PER):
            if n > 0:
                arrive(z_recv.at[n], z_base + n)
        block = z_recv[q * PER : (q + 1) * PER].reshape(128, WIDE)
        block = dot(to_blocks, block).astype(BF).reshape(PLANES, 16, WIDE)
        rows_buf[q, p] = block[:4]
        rows_send[q] = block[4:]
        row_gathers[q].start()

    def pack(v):
        left = iota((64, 128), 1) < 64
        return jnp.concatenate([v[:, :128], jnp.where(left, v[:64, 128:], v[64:, 128:])], axis=0)

    def multiply(q):
        row_gathers[q].finish()
        for side in (1, 0):
            gate = jnp.zeros((ROWS, 256), F32)
            upward = jnp.zeros((ROWS, 256), F32)
            for j in range(4):
                rows = rows_buf[q, :, j].reshape(ROWS, WIDE)
                cols = slice(j * WIDE, (j + 1) * WIDE)
                gate = gate + dot_t(rows, w_gate[side, :, cols])
                upward = upward + dot_t(rows, w_up[side, :, cols])
            if side == 1:
                sum_send[q, 0] = pack(gate).astype(BF)
                sum_send[q, 1] = pack(upward).astype(BF)
                send(sum_send.at[q], sum_recv.at[q], cross_sums[q], plane(1))
            else:
                sum_own[q, 0] = pack(gate)
                sum_own[q, 1] = pack(upward)

    def activate(q):
        arrive(sum_recv.at[q], cross_sums[q])
        gate = sum_own[q, 0] + sum_recv[q, 0].astype(F32)
        upward = sum_own[q, 1] + sum_recv[q, 1].astype(F32)
        hid[q, p] = (gate / (1.0 + jnp.exp(-gate)) * upward).astype(BF)
        hid_gathers[q].start()

    def finish_rows(q):
        hid_gathers[q].finish()
        left = iota((64, 128), 1) < 64
        result = [jnp.zeros((ROWS, 256), F32) for _ in (0, 1)]
        zero = jnp.zeros((64, 128), BF)
        for s in range(PLANES):
            tail = hid[q, s, 128:]
            tail = jnp.concatenate(
                [jnp.where(left, tail, zero), jnp.where(left, zero, tail)], axis=0
            )
            hidden = jnp.concatenate([hid[q, s, :128], tail], axis=1)
            for o in (0, 1):
                result[o] = result[o] + dot(hidden, w_down[o, s])
        for o in (0, 1):
            block = dot(to_requests, result[o].astype(BF)).astype(BF).reshape(PER, 16, 256)
            ret_send[q * PER : (q + 1) * PER, :, o * 256 : (o + 1) * 256] = block
        for n in range(q * PER, (q + 1) * PER):
            d, flip = slots[n]
            if n > 0:
                send(ret_send.at[n], ret.at[ex], ret_base + n, {"exp": exp_at(-d, flip)})
            else:
                ret[ex] = ret_send[0]

    gather_rows(0)
    pass_weights((0, 0 + 1))
    row_gathers[0].forward()
    pass_weights((2, 2 + 1))
    gather_rows(1)
    complete_weights()
    multiply(0)
    row_gathers[1].forward()
    gather_rows(2)
    activate(0)
    multiply(1)
    row_gathers[2].forward()
    hid_gathers[0].forward()
    gather_rows(3)
    activate(1)
    multiply(2)
    finish_rows(0)
    row_gathers[3].forward()
    hid_gathers[1].forward()
    activate(2)
    multiply(3)
    finish_rows(1)
    hid_gathers[2].forward()
    activate(3)
    finish_rows(2)
    hid_gathers[3].forward()

    for i in range(1, PLANES):
        arrive(info.at[peer[i]], info_base + peer[i])
    e_row, e_col = iota((128, 512), 0), iota((128, 512), 1)
    pick = onehot(e_row == (e_col >> 4))
    chosen = dot(info[:, 0].reshape(128, 128).astype(BF), pick)
    meets = (chosen == (e_col & 1).astype(F32)) & ((e_row >> 4) == ((e_col >> 1) & 7))
    mixing = [
        jnp.where(meets, dot(part, pick), 0.0).astype(BF)
        for part in thirds(info[:, 1].reshape(128, 128))
    ]

    finish_rows(3)
    for copy in started:
        copy.wait_send()
    started.clear()
    for n, (d, flip) in enumerate(slots):
        if n > 0:
            arrive(ret.at[exp_at(d, flip)], ret_base + n)
    returned = ret[...].reshape(512, WIDE)
    added = dot(mixing[0], returned) + dot(mixing[1], returned) + dot(mixing[2], returned)
    fin_send[...] = added.astype(BF).reshape(PLANES, TOK, WIDE)
    fin_base = take("recv", PLANES)
    for i in YS + (1, 3, 7, 5):
        send(fin_send.at[peer[i]], fin.at[p], fin_base + p, plane(i))
    fin[p] = fin_send[p]
    for i in range(1, PLANES):
        arrive(fin.at[peer[i]], fin_base + peer[i])
    for j in range(PLANES):
        total = stream_buf[j].astype(F32) + fin[j].astype(F32)
        out_ref[:, j * WIDE : (j + 1) * WIDE] = total.astype(BF)
    for copy in started:
        copy.wait_send()


def local(
    resid,
    query,
    key_new,
    value_new,
    cache_key,
    cache_value,
    cache_len,
    block_of,
    out_proj,
    norm_gain,
    routes,
    route_logits,
    w_gate,
    w_up,
    w_down,
):
    rates = np.exp(np.arange(HD // 2, dtype=np.float64) * (-2.0 * math.log(1000000.0) / HD))
    rates = jnp.asarray(np.concatenate([rates, rates])[None, :].astype(np.float32))
    vmem = pl.BlockSpec(memory_space=pltpu.VMEM)
    hbm = pl.BlockSpec(memory_space=pl.ANY)
    q_rows = 2 * GROUP * TOK
    scratch = [
        pltpu.SMEM((1,), jnp.int32),
        pltpu.SMEM((16,), jnp.int32),
        pltpu.VMEM((1, HD), F32),
        pltpu.VMEM((TOK, 4096), BF),
        pltpu.VMEM((TOK, 256), BF),
        pltpu.VMEM((TOK, 256), BF),
        pltpu.VMEM((CACHED, 256), BF),
        pltpu.VMEM((CACHED, 256), BF),
        pltpu.VMEM((TOK, 4096), BF),
        pltpu.VMEM((1, 4096), F32),
        pltpu.VMEM((8, TOK), jnp.int32),
        pltpu.VMEM((8, TOK), F32),
        pltpu.VMEM((q_rows, HD), BF),
        pltpu.VMEM((GROUP * TOK, HD), BF),
        pltpu.VMEM((PLANES, 2, 2, KEYS, HD), BF),
        pltpu.VMEM((2, KEYS, HD), BF),
        pltpu.VMEM((PLANES + 1, q_rows, 256), F32),
        pltpu.VMEM((q_rows, 128), F32),
        pltpu.VMEM((2, PLANES, TOK, 2048), BF),
        pltpu.VMEM((TOK, 2048), BF),
        pltpu.VMEM((2, 2, 2048, 256), BF),
        pltpu.VMEM((PLANES, TOK, WIDE), BF),
        pltpu.VMEM((PLANES, TOK, WIDE), BF),
        pltpu.VMEM((PLANES, TOK, WIDE), BF),
        pltpu.VMEM((PLANES, 2, TOK, 128), F32),
        pltpu.VMEM((NEXP, 16, WIDE), BF),
        pltpu.VMEM((NEXP, 16, WIDE), BF),
        pltpu.VMEM((CHUNKS, 4, 16, WIDE), BF),
        pltpu.VMEM((CHUNKS, PLANES, 4, 16, WIDE), BF),
        pltpu.VMEM((CHUNKS, 2, 192, 128), BF),
        pltpu.VMEM((CHUNKS, 2, 192, 128), BF),
        pltpu.VMEM((CHUNKS, 2, 192, 128), F32),
        pltpu.VMEM((2, 256, 2048), BF),
        pltpu.VMEM((2, 256, 2048), BF),
        pltpu.VMEM((2, PLANES, 256, 256), BF),
        pltpu.VMEM((CHUNKS, PLANES, 192, 128), BF),
        pltpu.VMEM((NEXP, 16, WIDE), BF),
        pltpu.VMEM((NEXP, 16, WIDE), BF),
        pltpu.VMEM((PLANES, TOK, WIDE), BF),
        pltpu.VMEM((PLANES, TOK, WIDE), BF),
        pltpu.SemaphoreType.DMA((SENDS,)),
        pltpu.SemaphoreType.DMA((RECVS,)),
        pltpu.SemaphoreType.DMA((16,)),
    ]
    out = pl.pallas_call(
        kernel,
        out_shape=jax.ShapeDtypeStruct((TOK, 4096), BF),
        in_specs=[hbm] * 16,
        out_specs=vmem,
        scratch_shapes=scratch,
        compiler_params=pltpu.CompilerParams(
            collective_id=0, has_side_effects=True, vmem_limit_bytes=56 * 2**20
        ),
        name="layer",
    )(
        cache_len,
        block_of,
        rates,
        query[0],
        key_new[0],
        value_new[0],
        cache_key[0],
        cache_value[0],
        resid[0],
        norm_gain[None, :],
        routes[0].T,
        route_logits[0].T,
        out_proj.reshape(2, 2048, 256),
        w_gate[0],
        w_up[0],
        w_down[0].reshape(PLANES, 192, 256),
    )
    return out[None]


def solution(mesh):
    rows = P("exp", "ctx", None)
    in_specs = (
        rows,
        rows,
        rows,
        rows,
        rows,
        rows,
        P("exp"),
        P(),
        P(None, "ctx"),
        P(),
        rows,
        rows,
        rows,
        rows,
        P("exp", None, "ctx"),
    )
    return jax.shard_map(local, mesh=mesh, in_specs=in_specs, out_specs=rows, check_vma=False)
```

```python
import math

import jax
import jax.numpy as jnp
import numpy as np
from jax import lax
from jax.experimental import pallas as pl
from jax.experimental.pallas import tpu as pltpu
from jax.sharding import PartitionSpec as P

MESH = pl.DeviceIdType.MESH
BF = jnp.bfloat16
F32 = jnp.float32
HD = 128
TOK = 16
CACHED = 128
KEYS = TOK + CACHED
GROUP = 16
PLANES = 8
WIDE = 512
NEXP = 32
UNITS = 96
OFFSETS = ((0, 1, -1, -2), (6, 5, -5, -4), (8, 7, -7, -6), (4, 3, -3, 2))
CHUNKS = len(OFFSETS)
PER = 8
ROWS = PER * 2 * PLANES
YS = (2, 6, 4)
NEG = -1e30
SENDS = 304
RECVS = 336


def iota(shape, axis):
    return lax.broadcasted_iota(jnp.int32, shape, axis)


def onehot(condition):
    return jnp.where(condition, 1.0, 0.0).astype(BF)


def dot(a, b):
    return jnp.dot(a, b, preferred_element_type=F32)


def dot_t(a, b):
    return lax.dot_general(a, b, (((1,), (1,)), ((), ())), preferred_element_type=F32)


def thirds(x):
    high = x.astype(BF)
    rest = x - high.astype(F32)
    middle = rest.astype(BF)
    return high, middle, (rest - middle.astype(F32)).astype(BF)


def kernel(
    length_hbm,
    block_hbm,
    rates_hbm,
    query_hbm,
    key_new_hbm,
    value_new_hbm,
    cache_key_hbm,
    cache_value_hbm,
    resid_hbm,
    gain_hbm,
    routes_hbm,
    logits_hbm,
    out_proj_hbm,
    gate_hbm,
    up_hbm,
    down_hbm,
    out_ref,
    length_ref,
    block_ref,
    rates_ref,
    query_ref,
    key_new_ref,
    value_new_ref,
    cache_key_ref,
    cache_value_ref,
    resid_ref,
    gain_ref,
    routes_ref,
    logits_ref,
    q_buf,
    q_stage,
    kv,
    kv_stage,
    score_buf,
    peak_buf,
    mix,
    mix_stage,
    w_out,
    proj_send,
    attn,
    stream_buf,
    info,
    z_send,
    z_recv,
    rows_send,
    rows_buf,
    sum_send,
    sum_recv,
    sum_own,
    w_gate,
    w_up,
    w_down,
    hid,
    ret_send,
    ret,
    fin_send,
    fin,
    send_sems,
    recv_sems,
    local_sems,
):
    ctx = lax.axis_index("ctx")
    ex = lax.axis_index("exp")
    core, p = lax.rem(ctx, 2), lax.div(ctx, 2)
    y, h = lax.div(p, 2), lax.rem(p, 2)
    z, low = lax.div(ex, 2), lax.rem(ex, 2)
    other = 1 - core
    ys = {0: y, 2: y + 1 - 2 * lax.rem(y, 2), 4: lax.rem(y + 2, 4), 6: 3 - y}
    peer = [2 * ys[i & 6] + ((1 - h) if i & 1 else h) for i in range(PLANES)]
    partner = {"ctx": 2 * p + other}

    def plane(i):
        return {"ctx": 2 * peer[i] + core}

    slots = []
    for chunk in OFFSETS:
        for d in chunk:
            for flip in (0, 1):
                slots.append((d, flip))

    def exp_at(d, flip):
        return 2 * lax.rem(z + d + 16, 16) + (1 - low if flip else low)

    started = []
    counts = {"send": 0, "recv": 0, "local": 0}

    def take(kind, n):
        first = counts[kind]
        counts[kind] += n
        assert counts[kind] <= {"send": SENDS, "recv": RECVS, "local": 16}[kind]
        return first

    def send(src, dst, recv, device):
        copy = pltpu.make_async_remote_copy(
            src_ref=src,
            dst_ref=dst,
            send_sem=send_sems.at[take("send", 1)],
            recv_sem=recv_sems.at[recv],
            device_id=device,
            device_id_type=MESH,
        )
        copy.start()
        started.append(copy)

    def arrive(dst, recv):
        pltpu.make_async_remote_copy(
            src_ref=dst,
            dst_ref=dst,
            send_sem=send_sems.at[0],
            recv_sem=recv_sems.at[recv],
            device_id=partner,
            device_id_type=MESH,
        ).wait_recv()

    class Gather:
        def __init__(self, at):
            self.at = at
            self.base = take("recv", 2 * PLANES)

        def put(self, source, half, i):
            ref = self.at(source, half)
            send(ref, ref, self.base + 2 * source + half, plane(i))

        def wait(self, i, half):
            arrive(self.at(peer[i], half), self.base + 2 * peer[i] + half)

        def start(self):
            self.put(p, 0, 1)
            for half in (0, 1):
                for i in YS:
                    self.put(p, half, i)
            self.put(p, 1, 1)

        def first(self):
            self.put(p, 0, 1)

        def rest(self):
            for half in (1, 0):
                for i in YS:
                    self.put(p, half, i)
            self.put(p, 1, 1)

        def forward(self):
            self.wait(1, 0)
            for i in YS:
                self.put(peer[1], 0, i)
            for i in YS:
                self.wait(i, 1)
                self.put(peer[i], 1, 1)

        def finish(self):
            for i in YS:
                self.wait(i, 0)
            self.wait(1, 1)
            for i in YS:
                self.wait(i + 1, 0)
                self.wait(i + 1, 1)

    class RowGather:
        def __init__(self, q):
            self.q = q
            self.base = take("recv", PLANES)

        def put(self, i, to):
            ref = rows_buf.at[self.q, peer[i]]
            send(ref, ref, self.base + peer[i], plane(to))

        def wait(self, i):
            arrive(rows_buf.at[self.q, peer[i]], self.base + peer[i])

        def start(self):
            send(rows_send.at[self.q], rows_buf.at[self.q, p], self.base + p, plane(1))
            for i in YS:
                self.put(0, i)

        def forward(self):
            self.wait(1)
            for i in YS:
                self.put(1, i)

        def finish(self):
            for i in YS + (3, 7, 5):
                self.wait(i)

    class Direct:
        def __init__(self, at):
            self.at = at
            self.base = take("recv", PLANES)

        def start(self):
            for i in YS + (1, 3, 7, 5):
                send(self.at(p), self.at(p), self.base + p, plane(i))

        def forward(self):
            pass

        def finish(self):
            for i in YS + (1, 3, 7, 5):
                arrive(self.at(peer[i]), self.base + peer[i])

    barrier = pltpu.get_barrier_semaphore()
    pl.semaphore_signal(barrier, inc=1, device_id=partner, device_id_type=MESH)
    for i in range(1, PLANES):
        pl.semaphore_signal(barrier, inc=1, device_id=plane(i), device_id_type=MESH)
    for d, flip in slots[1:]:
        pl.semaphore_signal(
            barrier, inc=1, device_id={"exp": exp_at(d, flip)}, device_id_type=MESH
        )

    loads = []
    for src, dst in (
        (length_hbm, length_ref),
        (block_hbm, block_ref),
        (cache_key_hbm, cache_key_ref),
        (cache_value_hbm, cache_value_ref),
        (rates_hbm, rates_ref),
        (key_new_hbm, key_new_ref),
        (value_new_hbm, value_new_ref),
        (query_hbm, query_ref),
        (routes_hbm, routes_ref),
        (logits_hbm, logits_ref),
        (resid_hbm, resid_ref),
        (gain_hbm, gain_ref),
    ):
        copy = pltpu.make_async_copy(src, dst, local_sems.at[take("local", 1)])
        copy.start()
        loads.append(copy)
    mine96 = pl.ds(pl.multiple_of(core * UNITS, 16), UNITS)
    head192 = pl.ds(0, 2 * UNITS)
    near_cols = pl.ds(pl.multiple_of(h * 2048, 2048), 2048)
    far_cols = pl.ds(pl.multiple_of((1 - h) * 2048, 2048), 2048)
    locals_ = []
    for src, dst in (
        (out_proj_hbm, w_out.at[core]),
        (gate_hbm.at[:, near_cols], w_gate.at[0, mine96]),
        (up_hbm.at[:, near_cols], w_up.at[0, mine96]),
        (down_hbm, w_down.at[core, :, head192]),
    ):
        copy = pltpu.make_async_copy(src, dst, local_sems.at[take("local", 1)])
        copy.start()
        locals_.append(copy)

    first = core == 0
    for copy in loads[:2]:
        copy.wait()
    length = length_ref[0]
    block_mine = block_ref[ctx]
    block_other = block_ref[2 * p + other]
    position = (iota((TOK, HD), 0) + (length + block_mine * TOK)).astype(F32)

    def rope(v):
        v = v.astype(F32)
        return (v * cosine + pltpu.roll(v, HD // 2, 1) * sine).astype(BF)

    for copy in loads[2:10]:
        copy.wait()
    angles = position * rates_ref[...]
    cosine = jnp.cos(angles)
    sine = jnp.where(iota((TOK, HD), 1) < HD // 2, -1.0, 1.0) * jnp.sin(angles)
    for g in range(GROUP):
        low_head = rope(query_ref[:, g * HD : (g + 1) * HD])
        high_head = rope(query_ref[:, (GROUP + g) * HD : (GROUP + g + 1) * HD])
        q_buf[g * TOK : (g + 1) * TOK] = jnp.where(first, low_head, high_head)
        q_stage[g * TOK : (g + 1) * TOK] = jnp.where(first, high_head, low_head)
    for which, cached_ref, new_ref in ((0, cache_key_ref, key_new_ref), (1, cache_value_ref, value_new_ref)):
        old = [cached_ref[:, n * HD : (n + 1) * HD] for n in (0, 1)]
        new = [new_ref[:, n * HD : (n + 1) * HD] for n in (0, 1)]
        if which == 0:
            new = [rope(v) for v in new]
        kv[p, 0, which, :CACHED] = jnp.where(first, old[0], old[1])
        kv[p, 0, which, CACHED:] = jnp.where(first, new[0], new[1])
        kv_stage[which, :CACHED] = jnp.where(first, old[1], old[0])
        kv_stage[which, CACHED:] = jnp.where(first, new[1], new[0])

    logits = logits_ref[...]
    powers = jnp.exp(logits - jnp.max(logits, axis=0, keepdims=True))
    shares = powers / jnp.sum(powers, axis=0, keepdims=True)
    routes = jnp.concatenate([routes_ref[...], jnp.full((8, 128 - TOK), -1, jnp.int32)], axis=1)
    shares = jnp.concatenate([shares, jnp.zeros((8, 128 - TOK), F32)], axis=1)
    expert = iota((NEXP, 128), 0)
    token = iota((NEXP, 128), 1)
    taken = jnp.zeros((NEXP, 128), F32)
    share = jnp.zeros((NEXP, 128), F32)
    for x in range(8):
        hit = routes[x : x + 1] == expert
        taken = jnp.where(hit, 1.0, taken)
        share = share + jnp.where(hit, shares[x : x + 1], 0.0)
    rank = taken
    for step in (1, 2, 4, 8):
        rank = rank + jnp.where(token >= step, pltpu.roll(rank, step, 1), 0.0)
    row_of = jnp.where(taken > 0.0, rank - 1.0, -1.0)
    rest = jnp.zeros((128 - NEXP, 128), F32)
    row_of = jnp.concatenate([row_of, rest], axis=0).T[:TOK]
    share = jnp.concatenate([share, rest], axis=0).T[:TOK]
    info[p, 0] = row_of
    info[p, 1] = share

    pl.semaphore_wait(barrier, PLANES + len(slots) - 1)

    kv_gather = Gather(lambda source, half: kv.at[source, half])
    pair_kv, pair_q = take("recv", 1), take("recv", 1)
    send(kv_stage, kv.at[p, 1], pair_kv, partner)
    kv_gather.first()
    q_theirs = q_buf.at[pl.ds(GROUP * TOK, GROUP * TOK)]
    send(q_stage, q_theirs, pair_q, partner)
    arrive(kv.at[p, 1], pair_kv)
    kv_gather.rest()
    pair_weights = [take("recv", 1) for _ in range(4)]
    send(out_proj_hbm, w_out.at[core], pair_weights[0], partner)
    send(gate_hbm.at[:, near_cols], w_gate.at[0, mine96], pair_weights[1], partner)
    send(up_hbm.at[:, near_cols], w_up.at[0, mine96], pair_weights[2], partner)
    send(down_hbm, w_down.at[core, :, head192], pair_weights[3], partner)
    cross_weights = [take("recv", 1) for _ in range(8)]

    def cross(piece):
        src, dst = ((gate_hbm, w_gate), (up_hbm, w_up))[piece // 2]
        rows = pl.ds(48 * (piece % 2), 48)
        to = pl.ds(pl.multiple_of(core * UNITS + 48 * (piece % 2), 16), 48)
        send(src.at[rows, far_cols], dst.at[1, to], cross_weights[piece], plane(1))

    def crossed(piece, whose):
        dst = (w_gate, w_up)[piece // 2]
        return dst.at[1, pl.ds(pl.multiple_of(whose * UNITS + 48 * (piece % 2), 16), 48)]

    info_base = take("recv", PLANES)
    for i in range(1, PLANES):
        send(info.at[p], info.at[p], info_base + p, plane(i))

    row8 = jnp.concatenate([row_of.astype(BF)] * PLANES, axis=0)
    s_row, s_lane = iota((512, 128), 0), iota((512, 128), 1)
    spread = dot_t(onehot((s_row >> 4) == s_lane), row8)
    select = onehot(
        (spread == ((s_row >> 3) & 1).astype(F32)) & ((s_row & 7) == (s_lane >> 4))
    )

    scale = HD ** (-0.5)
    arrive(q_theirs, pair_q)
    q_rows = 2 * GROUP * TOK
    QB = 128

    key_lane = iota((1, 256), 1)

    def score(slot, keys, visible_of):
        def step(rb, carry):
            rows = pl.ds(pl.multiple_of(rb * QB, QB), QB)
            s = dot_t(q_buf[rows], keys) * scale
            s = jnp.where(visible_of(rb), s, NEG)
            score_buf[slot, rows] = s
            top = jnp.maximum(s[:, :128], s[:, 128:])
            peak_buf[rows] = jnp.maximum(peak_buf[rows], top)
            return carry

        lax.fori_loop(0, q_rows // QB, step, 0)

    def score_cached(i):
        source = peer[i]
        keys = jnp.concatenate([kv[source, 0, 0, :CACHED], kv[source, 1, 0, :CACHED]], axis=0)
        near = (2 * source + core) * CACHED
        far = (2 * source + other) * CACHED
        slot = jnp.where(key_lane < CACHED, near + key_lane, far + key_lane - CACHED)
        visible = slot < length
        score(source, keys, lambda rb: visible)

    peak_buf[...] = jnp.full((q_rows, 128), NEG, F32)
    score_cached(0)
    kv_gather.forward()
    cross(0)
    cross(1)
    for i in YS:
        kv_gather.wait(i, 0)
        score_cached(i)
    kv_gather.wait(1, 1)
    score_cached(1)
    for i in (3, 7, 5):
        kv_gather.wait(i, 0)
        kv_gather.wait(i, 1)
        score_cached(i)
    new_keys = jnp.concatenate(
        [kv[s, o, 0, CACHED:] for s in range(PLANES) for o in (0, 1)], axis=0
    )
    new_values = jnp.concatenate(
        [kv[s, o, 1, CACHED:] for s in range(PLANES) for o in (0, 1)], axis=0
    )
    key_offset = jnp.zeros((1, 256), jnp.int32)
    for s in range(PLANES):
        for o in (0, 1):
            block = block_ref[2 * s + (core if o == 0 else other)]
            key_offset = jnp.where((key_lane >> 4) == 2 * s + o, block * TOK, key_offset)
    key_offset = key_offset + (key_lane & 15)

    def causal(rb):
        block = jnp.where(rb < 2, block_mine, block_other)
        return key_offset <= (iota((QB, 256), 0) & 15) + block * TOK

    score(PLANES, new_keys, causal)

    def weigh(rb, carry):
        rows = pl.ds(pl.multiple_of(rb * QB, QB), QB)
        peak = jnp.max(peak_buf[rows], axis=1, keepdims=True)
        total = jnp.zeros((QB, 128), F32)
        mixed = jnp.zeros((QB, HD), F32)
        for s in range(PLANES + 1):
            weights = jnp.exp(score_buf[s, rows] - peak)
            total = total + weights[:, :128] + weights[:, 128:]
            if s < PLANES:
                values = jnp.concatenate([kv[s, 0, 1, :CACHED], kv[s, 1, 1, :CACHED]], axis=0)
            else:
                values = new_values
            mixed = mixed + dot(weights.astype(BF), values)
        mixed = (mixed / jnp.sum(total, axis=1, keepdims=True)).astype(BF)
        q_buf[rows] = mixed
        return carry

    def mix_half(o, ref):
        lax.fori_loop(2 * o, 2 * o + 2, weigh, 0)
        for g in range(GROUP):
            r = (o * GROUP + g) * TOK
            ref[:, g * HD : (g + 1) * HD] = q_buf[r : r + TOK]

    pair_mix = take("recv", 1)
    mix_gather = Gather(lambda source, half: mix.at[half, source])
    mix_half(1, mix_stage)
    send(mix_stage, mix.at[1, p], pair_mix, partner)
    mix_half(0, mix.at[0, p])
    mix_gather.first()
    arrive(mix.at[1, p], pair_mix)
    mix_gather.rest()
    mix_gather.forward()
    locals_[0].wait()
    arrive(w_out.at[other], pair_weights[0])
    for i in YS + (3, 7, 5):
        mix_gather.wait(i, 0)
    left = mix[0].reshape(PLANES * TOK, 2048)
    projected = [dot(left, w_out[o, core]) for o in (0, 1)]
    for i in (1, 3, 7, 5):
        mix_gather.wait(i, 1)
    left = mix[1].reshape(PLANES * TOK, 2048)
    for o in (0, 1):
        block = projected[o] + dot(left, w_out[o, other])
        proj_send[:, :, o * 256 : (o + 1) * 256] = block.astype(BF).reshape(PLANES, TOK, 256)
    attn_base = take("recv", PLANES)
    for i in YS + (1, 3, 7, 5):
        send(proj_send.at[peer[i]], attn.at[p], attn_base + p, plane(i))
    cross(2)
    attn[p] = proj_send[p]
    for i in range(1, PLANES):
        arrive(attn.at[peer[i]], attn_base + peer[i])

    for copy in loads[10:]:
        copy.wait()
    square = jnp.zeros((TOK, 1), F32)
    streams = []
    for j in range(PLANES):
        cols = slice(j * WIDE, (j + 1) * WIDE)
        v = (resid_ref[:, cols].astype(F32) + attn[j].astype(F32)).astype(BF)
        stream_buf[j] = v
        v = v.astype(F32)
        streams.append(v)
        square = square + jnp.sum(v * v, axis=1, keepdims=True)
    inverse = lax.rsqrt(square * (1.0 / (PLANES * WIDE)) + 1e-06)
    normed = jnp.concatenate(
        [
            (streams[j] * inverse * gain_ref[:, j * WIDE : (j + 1) * WIDE]).astype(BF)
            for j in range(PLANES)
        ],
        axis=0,
    )
    z_send[...] = dot(select, normed).astype(BF).reshape(NEXP, 16, WIDE)

    z_base = take("recv", len(slots))
    z_recv[0] = z_send[ex]
    for n, (d, flip) in enumerate(slots):
        if n > 0:
            to = exp_at(d, flip)
            send(z_send.at[to], z_recv.at[n], z_base + n, {"exp": to})
        if n == PER - 1:
            cross(3)

    theirs96 = pl.ds(pl.multiple_of(other * UNITS, 16), UNITS)

    def pass_weights(pieces):
        for piece in pieces:
            ref = crossed(piece, core)
            arrive(ref, cross_weights[piece])
            send(ref, ref, cross_weights[4 + piece], partner)

    def complete_weights():
        for copy in locals_[1:]:
            copy.wait()
        arrive(w_gate.at[0, theirs96], pair_weights[1])
        arrive(w_up.at[0, theirs96], pair_weights[2])
        arrive(w_down.at[other, :, head192], pair_weights[3])
        for piece in range(4):
            arrive(crossed(piece, other), cross_weights[4 + piece])
        for side in (0, 1):
            w_gate[side, 192:] = w_gate[side, 128:192]
            w_up[side, 192:] = w_up[side, 128:192]
        for o in (0, 1):
            w_down[o, :, 192:] = w_down[o, :, 128:192]

    r_, c_ = iota((128, 128), 0), iota((128, 128), 1)
    to_blocks = onehot(((((r_ >> 4) + 4 * h) & 7) == (c_ & 7)) & ((r_ & 15) == (c_ >> 3)))
    to_requests = onehot(
        ((r_ >> 4) == ((c_ >> 1) & 7)) & (((r_ >> 1) & 7) == (c_ >> 4)) & ((r_ & 1) == (c_ & 1))
    )
    ret_base = take("recv", len(slots))
    row_gathers = [RowGather(q) for q in range(CHUNKS)]
    cross_sums = [take("recv", 1) for _ in range(CHUNKS)]
    hid_gathers = [
        Gather(lambda source, half, q=q: hid.at[q, source, pl.ds(UNITS * half, UNITS)])
        for q in range(CHUNKS - 1)
    ]
    hid_gathers.append(Direct(lambda source: hid.at[CHUNKS - 1, source]))

    def gather_rows(q):
        for n in range(q * PER, (q + 1) * PER):
            if n > 0:
                arrive(z_recv.at[n], z_base + n)
        block = z_recv[q * PER : (q + 1) * PER].reshape(128, WIDE)
        block = dot(to_blocks, block).astype(BF).reshape(PLANES, 16, WIDE)
        rows_buf[q, p] = block[:4]
        rows_send[q] = block[4:]
        row_gathers[q].start()

    def pack(v):
        left = iota((64, 128), 1) < 64
        return jnp.concatenate([v[:, :128], jnp.where(left, v[:64, 128:], v[64:, 128:])], axis=0)

    def multiply(q, side):
        if side == 1:
            row_gathers[q].finish()
        for side in (side,):
            gate = jnp.zeros((ROWS, 256), F32)
            upward = jnp.zeros((ROWS, 256), F32)
            for j in range(4):
                rows = rows_buf[q, :, j].reshape(ROWS, WIDE)
                cols = slice(j * WIDE, (j + 1) * WIDE)
                gate = gate + dot_t(rows, w_gate[side, :, cols])
                upward = upward + dot_t(rows, w_up[side, :, cols])
            if side == 1:
                sum_send[q, 0] = pack(gate).astype(BF)
                sum_send[q, 1] = pack(upward).astype(BF)
                send(sum_send.at[q], sum_recv.at[q], cross_sums[q], plane(1))
            else:
                sum_own[q, 0] = pack(gate)
                sum_own[q, 1] = pack(upward)

    def activate(q):
        arrive(sum_recv.at[q], cross_sums[q])
        gate = sum_own[q, 0] + sum_recv[q, 0].astype(F32)
        upward = sum_own[q, 1] + sum_recv[q, 1].astype(F32)
        hid[q, p] = (gate / (1.0 + jnp.exp(-gate)) * upward).astype(BF)
        hid_gathers[q].start()

    def finish_rows(q):
        hid_gathers[q].finish()
        left = iota((64, 128), 1) < 64
        result = [jnp.zeros((ROWS, 256), F32) for _ in (0, 1)]
        zero = jnp.zeros((64, 128), BF)
        for s in range(PLANES):
            tail = hid[q, s, 128:]
            tail = jnp.concatenate(
                [jnp.where(left, tail, zero), jnp.where(left, zero, tail)], axis=0
            )
            hidden = jnp.concatenate([hid[q, s, :128], tail], axis=1)
            for o in (0, 1):
                result[o] = result[o] + dot(hidden, w_down[o, s])
        for o in (0, 1):
            block = dot(to_requests, result[o].astype(BF)).astype(BF).reshape(PER, 16, 256)
            ret_send[q * PER : (q + 1) * PER, :, o * 256 : (o + 1) * 256] = block
        for n in range(q * PER, (q + 1) * PER):
            d, flip = slots[n]
            if n > 0:
                send(ret_send.at[n], ret.at[ex], ret_base + n, {"exp": exp_at(-d, flip)})
            else:
                ret[ex] = ret_send[0]

    gather_rows(0)
    pass_weights((0, 0 + 1))
    row_gathers[0].forward()
    pass_weights((2, 2 + 1))
    gather_rows(1)
    complete_weights()
    multiply(0, 1)
    row_gathers[1].forward()
    multiply(0, 0)
    gather_rows(2)
    activate(0)
    multiply(1, 1)
    row_gathers[2].forward()
    multiply(1, 0)
    hid_gathers[0].forward()
    gather_rows(3)
    activate(1)
    multiply(2, 1)
    row_gathers[3].forward()
    multiply(2, 0)
    finish_rows(0)
    hid_gathers[1].forward()
    activate(2)
    multiply(3, 1)
    multiply(3, 0)
    finish_rows(1)
    hid_gathers[2].forward()
    activate(3)
    finish_rows(2)
    hid_gathers[3].forward()

    for i in range(1, PLANES):
        arrive(info.at[peer[i]], info_base + peer[i])
    e_row, e_col = iota((128, 512), 0), iota((128, 512), 1)
    pick = onehot(e_row == (e_col >> 4))
    chosen = dot(info[:, 0].reshape(128, 128).astype(BF), pick)
    meets = (chosen == (e_col & 1).astype(F32)) & ((e_row >> 4) == ((e_col >> 1) & 7))
    mixing = [
        jnp.where(meets, dot(part, pick), 0.0).astype(BF)
        for part in thirds(info[:, 1].reshape(128, 128))
    ]

    finish_rows(3)
    for copy in started:
        copy.wait_send()
    started.clear()
    for n, (d, flip) in enumerate(slots):
        if n > 0:
            arrive(ret.at[exp_at(d, flip)], ret_base + n)
    returned = ret[...].reshape(512, WIDE)
    added = dot(mixing[0], returned) + dot(mixing[1], returned) + dot(mixing[2], returned)
    fin_send[...] = added.astype(BF).reshape(PLANES, TOK, WIDE)
    fin_base = take("recv", PLANES)
    for i in YS + (1, 3, 7, 5):
        send(fin_send.at[peer[i]], fin.at[p], fin_base + p, plane(i))
    fin[p] = fin_send[p]
    for i in range(1, PLANES):
        arrive(fin.at[peer[i]], fin_base + peer[i])
    for j in range(PLANES):
        total = stream_buf[j].astype(F32) + fin[j].astype(F32)
        out_ref[:, j * WIDE : (j + 1) * WIDE] = total.astype(BF)
    for copy in started:
        copy.wait_send()


def local(
    resid,
    query,
    key_new,
    value_new,
    cache_key,
    cache_value,
    cache_len,
    block_of,
    out_proj,
    norm_gain,
    routes,
    route_logits,
    w_gate,
    w_up,
    w_down,
):
    rates = np.exp(np.arange(HD // 2, dtype=np.float64) * (-2.0 * math.log(1000000.0) / HD))
    rates = jnp.asarray(np.concatenate([rates, rates])[None, :].astype(np.float32))
    vmem = pl.BlockSpec(memory_space=pltpu.VMEM)
    hbm = pl.BlockSpec(memory_space=pl.ANY)
    q_rows = 2 * GROUP * TOK
    scratch = [
        pltpu.SMEM((1,), jnp.int32),
        pltpu.SMEM((16,), jnp.int32),
        pltpu.VMEM((1, HD), F32),
        pltpu.VMEM((TOK, 4096), BF),
        pltpu.VMEM((TOK, 256), BF),
        pltpu.VMEM((TOK, 256), BF),
        pltpu.VMEM((CACHED, 256), BF),
        pltpu.VMEM((CACHED, 256), BF),
        pltpu.VMEM((TOK, 4096), BF),
        pltpu.VMEM((1, 4096), F32),
        pltpu.VMEM((8, TOK), jnp.int32),
        pltpu.VMEM((8, TOK), F32),
        pltpu.VMEM((q_rows, HD), BF),
        pltpu.VMEM((GROUP * TOK, HD), BF),
        pltpu.VMEM((PLANES, 2, 2, KEYS, HD), BF),
        pltpu.VMEM((2, KEYS, HD), BF),
        pltpu.VMEM((PLANES + 1, q_rows, 256), F32),
        pltpu.VMEM((q_rows, 128), F32),
        pltpu.VMEM((2, PLANES, TOK, 2048), BF),
        pltpu.VMEM((TOK, 2048), BF),
        pltpu.VMEM((2, 2, 2048, 256), BF),
        pltpu.VMEM((PLANES, TOK, WIDE), BF),
        pltpu.VMEM((PLANES, TOK, WIDE), BF),
        pltpu.VMEM((PLANES, TOK, WIDE), BF),
        pltpu.VMEM((PLANES, 2, TOK, 128), F32),
        pltpu.VMEM((NEXP, 16, WIDE), BF),
        pltpu.VMEM((NEXP, 16, WIDE), BF),
        pltpu.VMEM((CHUNKS, 4, 16, WIDE), BF),
        pltpu.VMEM((CHUNKS, PLANES, 4, 16, WIDE), BF),
        pltpu.VMEM((CHUNKS, 2, 192, 128), BF),
        pltpu.VMEM((CHUNKS, 2, 192, 128), BF),
        pltpu.VMEM((CHUNKS, 2, 192, 128), F32),
        pltpu.VMEM((2, 256, 2048), BF),
        pltpu.VMEM((2, 256, 2048), BF),
        pltpu.VMEM((2, PLANES, 256, 256), BF),
        pltpu.VMEM((CHUNKS, PLANES, 192, 128), BF),
        pltpu.VMEM((NEXP, 16, WIDE), BF),
        pltpu.VMEM((NEXP, 16, WIDE), BF),
        pltpu.VMEM((PLANES, TOK, WIDE), BF),
        pltpu.VMEM((PLANES, TOK, WIDE), BF),
        pltpu.SemaphoreType.DMA((SENDS,)),
        pltpu.SemaphoreType.DMA((RECVS,)),
        pltpu.SemaphoreType.DMA((16,)),
    ]
    out = pl.pallas_call(
        kernel,
        out_shape=jax.ShapeDtypeStruct((TOK, 4096), BF),
        in_specs=[hbm] * 16,
        out_specs=vmem,
        scratch_shapes=scratch,
        compiler_params=pltpu.CompilerParams(
            collective_id=0, has_side_effects=True, vmem_limit_bytes=56 * 2**20
        ),
        name="layer",
    )(
        cache_len,
        block_of,
        rates,
        query[0],
        key_new[0],
        value_new[0],
        cache_key[0],
        cache_value[0],
        resid[0],
        norm_gain[None, :],
        routes[0].T,
        route_logits[0].T,
        out_proj.reshape(2, 2048, 256),
        w_gate[0],
        w_up[0],
        w_down[0].reshape(PLANES, 192, 256),
    )
    return out[None]


def solution(mesh):
    rows = P("exp", "ctx", None)
    in_specs = (
        rows,
        rows,
        rows,
        rows,
        rows,
        rows,
        P("exp"),
        P(),
        P(None, "ctx"),
        P(),
        rows,
        rows,
        rows,
        rows,
        P("exp", None, "ctx"),
    )
    return jax.shard_map(local, mesh=mesh, in_specs=in_specs, out_specs=rows, check_vma=False)
```
